32 devices in a mesh: replica: 4 (over x, core), fsdp: 8 (over z, y).
Axes of the slice: x: 2, y: 2, z: 4, core: 2. Of those that a mesh axis runs over, the one named last changes fastest.
Arguments:
- pseudo_grad: bfloat16 [4, 256, 8192], P('replica', 'fsdp'), may hold values from -400 to 400
- params: float32 [256, 8192], P('fsdp'), may hold values from -6 to 6
- momentum: float32 [256, 8192], P('fsdp'), may hold values from -6 to 6
Outputs:
- new_params: float32 [256, 8192], P('fsdp')
- new_momentum: float32 [256, 8192], P('fsdp')
The draws below stay inside these ranges and needn't reach their ends.
All inputs are finite; a program needn't handle non-finite values.
Results may differ from the reference program's by a relative error of at most 0.0003.
Values may be sent and summed in bfloat16 or wider, within the bound.
No kernel may reach another device: no remote copies, remote signals or barrier semaphores. Data moves between devices by JAX's collectives and lax.ppermute only.
A program may use at most 64 MiB of HBM per device.

```python
import jax
import jax.numpy as jnp
from jax import lax

D = 8192
ROWS = 256
REPLICAS = 4


def column_signs(key):
    coins = jax.random.bernoulli(key, 0.5, (REPLICAS, 1, D))
    return jnp.where(coins, 1.0, -1.0).astype(jnp.float32)


def draw_pseudo_grad(key, part):
    key = jax.random.fold_in(key, 7)
    key_sign, key_common, key_own = jax.random.split(key, 3)
    rows_pos = jnp.arange(ROWS, dtype=jnp.float32) / ROWS
    cols_pos = jnp.arange(D, dtype=jnp.float32) / D
    signs = column_signs(key_sign)
    scale = (10.0 ** rows_pos)[:, None] * (10.0 ** cols_pos)[None, :]
    common = jax.random.normal(key_common, (ROWS, D), jnp.float32)
    own = jax.random.normal(key_own, (REPLICAS, ROWS, D), jnp.float32)
    values = (0.9 * signs * common[None] + 0.45 * own) * scale[None]
    values = jnp.clip(values, -400.0, 400.0)
    return values.astype(jnp.bfloat16)


def levels(key, extent, shards, low, top_value):
    loudness = 1.0
    for dim, blocks in shards:
        steps = jax.random.uniform(jax.random.fold_in(jax.random.fold_in(key, 6), dim), (blocks,), jnp.float32, low / len(shards), top_value / len(shards))
        loudness = loudness * jnp.repeat(jnp.exp(steps), extent[dim] // blocks).reshape((-1,) + (1,) * (len(extent) - 1 - dim))
    return loudness


def gaussian(rng, dims, spread, reach, shards=(), held_as=jnp.bfloat16):
    values = spread * jax.random.normal(rng, dims, jnp.float32)
    if shards:
        values = values * levels(rng, dims, shards, -0.22, 0.18)
    return jnp.clip(values, -reach, reach).astype(held_as)


def setup_inputs(seed: int = 0) -> dict:
    arg_keys = jax.random.split(jax.random.key(seed), 4)
    pseudo_grad = draw_pseudo_grad(jax.random.fold_in(arg_keys[3], 71), 0)
    params = gaussian(arg_keys[1], (ROWS, D), 1.0, 6.0, ((0, 8),), jnp.float32)
    momentum = gaussian(arg_keys[2], (ROWS, D), 0.5, 6.0, ((0, 8),), jnp.float32)
    return dict(pseudo_grad=pseudo_grad, params=params, momentum=momentum)


def reference(pseudo_grad, params, momentum):
    total = lax.optimization_barrier(jnp.sum(pseudo_grad.astype(jnp.float32), axis=0))
    average = total / jnp.float32(REPLICAS)
    row_squares = lax.optimization_barrier(jnp.sum(average * average, axis=1))
    mean_sq = jnp.sum(row_squares) / jnp.float32(ROWS * D)
    rms = jnp.sqrt(mean_sq + 1e-06)
    factor = 0.2 / rms
    clipped = factor * average
    new_momentum = 0.9 * momentum + clipped
    new_params = params - 0.7 * (clipped + 0.9 * new_momentum)
    return (new_params, new_momentum)
```

```python
import jax
import jax.numpy as jnp
from jax import lax
from jax.sharding import PartitionSpec as P


def swapped(value, axis, flip):
    size = lax.axis_size(axis)
    return lax.ppermute(value, axis, [(i, i ^ flip) for i in range(size)])


def replica_total(grad):
    size = lax.axis_size("replica")
    wide = jnp.float32
    if size & (size - 1):
        return lax.psum(grad.astype(wide), "replica")
    if size == 1:
        return grad.astype(wide)
    mate = swapped(grad, "replica", 1)
    total = grad.astype(wide) + mate.astype(wide)
    if size >= 4:
        across = swapped(grad, "replica", 2)
        beyond = swapped(across, "replica", 1)
        total = total + (across.astype(wide) + beyond.astype(wide))
    step = 4
    while step < size:
        total = total + swapped(total, "replica", step)
        step *= 2
    return total


def fsdp_sum(value):
    size = lax.axis_size("fsdp")
    if size & (size - 1):
        return lax.psum(value, "fsdp")
    step = 1
    while step < size:
        radix = min(8, size // step)
        parts = [value] + [swapped(value, "fsdp", step * k) for k in range(1, radix)]
        while len(parts) > 1:
            parts = [parts[i] + parts[i + 1] for i in range(0, len(parts), 2)]
        value = parts[0]
        step *= radix
    return value


def per_device(pseudo_grad, params, momentum):
    groups = lax.axis_size("replica")
    count = params.shape[0] * lax.axis_size("fsdp") * params.shape[1]
    average = replica_total(pseudo_grad[0]) / jnp.float32(groups)
    square_sum = fsdp_sum(jnp.sum(jnp.sum(average * average, axis=1)))
    rms = jnp.sqrt(square_sum / jnp.float32(count) + 1e-06)
    clipped = (0.2 / rms) * average
    new_momentum = 0.9 * momentum + clipped
    new_params = params - 0.7 * (clipped + 0.9 * new_momentum)
    return (new_params, new_momentum)


def solution(mesh):
    placed = (P("replica", "fsdp", None), P("fsdp", None), P("fsdp", None))
    return jax.shard_map(
        per_device,
        mesh=mesh,
        in_specs=placed,
        out_specs=(P("fsdp", None), P("fsdp", None)),
        check_vma=False,
    )
```

```python
import jax
import jax.numpy as jnp
from jax import lax
from jax.sharding import PartitionSpec as P


def swapped(value, axis, flip):
    size = lax.axis_size(axis)
    return lax.ppermute(value, axis, [(i, i ^ flip) for i in range(size)])


def replica_total(grad):
    size = lax.axis_size("replica")
    wide = jnp.float32
    if size & (size - 1):
        return lax.psum(grad.astype(wide), "replica")
    if size == 1:
        return grad.astype(wide)
    mate = swapped(grad, "replica", 1)
    total = grad.astype(wide) + mate.astype(wide)
    if size >= 4:
        across = swapped(grad, "replica", 2)
        beyond = swapped(across, "replica", 1)
        total = total + (across.astype(wide) + beyond.astype(wide))
    step = 4
    while step < size:
        total = total + swapped(total, "replica", step)
        step *= 2
    return total


def fsdp_sum(value):
    size = lax.axis_size("fsdp")
    copies = jnp.broadcast_to(value, (size, 1, 128))
    parts = lax.all_to_all(copies, "fsdp", split_axis=0, concat_axis=0, tiled=True)
    return jnp.sum(parts[:, 0, 0])


def per_device(pseudo_grad, params, momentum):
    groups = lax.axis_size("replica")
    count = params.shape[0] * lax.axis_size("fsdp") * params.shape[1]
    average = replica_total(pseudo_grad[0]) / jnp.float32(groups)
    square_sum = fsdp_sum(jnp.sum(jnp.sum(average * average, axis=1)))
    rms = jnp.sqrt(square_sum / jnp.float32(count) + 1e-06)
    clipped = (0.2 / rms) * average
    new_momentum = 0.9 * momentum + clipped
    new_params = params - 0.7 * (clipped + 0.9 * new_momentum)
    return (new_params, new_momentum)


def solution(mesh):
    placed = (P("replica", "fsdp", None), P("fsdp", None), P("fsdp", None))
    return jax.shard_map(
        per_device,
        mesh=mesh,
        in_specs=placed,
        out_specs=(P("fsdp", None), P("fsdp", None)),
        check_vma=False,
    )
```

```python
import functools

import jax
import jax.numpy as jnp
from jax import lax
from jax.experimental import pallas as pl
from jax.experimental.pallas import tpu as pltpu
from jax.sharding import PartitionSpec as P

WIDE = jnp.float32
VMEM = pl.BlockSpec(memory_space=pltpu.VMEM)
HBM = pl.BlockSpec(memory_space=pltpu.HBM)
LIMIT = 16 * 1024 * 1024


def swapped(value, axis, flip):
    size = lax.axis_size(axis)
    return lax.ppermute(value, axis, [(i, i ^ flip) for i in range(size)])


def piece_of(k, width):
    return pl.ds(pl.multiple_of((lax.axis_index("replica") ^ k) * width, width), width)


def tree(parts):
    while len(parts) > 1:
        parts = [parts[i] + parts[i + 1] for i in range(0, len(parts), 2)]
    return parts[0]


def cut_kernel(grad, *rest):
    pieces, sems = rest[:-1], rest[-1]
    width = pieces[0].shape[1]
    copies = [
        pltpu.make_async_copy(grad.at[0, :, piece_of(k, width)], piece, sems.at[k])
        for k, piece in enumerate(pieces)
    ]
    for copy in copies:
        copy.start()
    for copy in copies:
        copy.wait()


def average_kernel(*refs):
    pieces, (average, squares) = refs[:-2], refs[-2:]
    total = tree([piece[...].astype(WIDE) for piece in pieces])
    mean = total / WIDE(len(pieces))
    average[...] = mean
    row = jnp.sum(mean * mean, axis=0, keepdims=True)
    lanes = functools.reduce(
        jnp.add, [row[:, i : i + 128] for i in range(0, row.shape[1], 128)]
    )
    squares[...] = jnp.broadcast_to(lanes[None], squares.shape)


def update_kernel(count, squares, params, momentum, *refs):
    averages, (new_params, new_momentum) = refs[:-2], refs[-2:]
    square_sum = jnp.sum(squares[...], keepdims=True).reshape(1, 1)
    factor = 0.2 / jnp.sqrt(square_sum / WIDE(count) + 1e-06)
    width = averages[0].shape[1]
    for k, average in enumerate(averages):
        cols = piece_of(k, width)
        clipped = factor * average[...]
        fresh = 0.9 * momentum[:, cols] + clipped
        new_momentum[:, cols] = fresh
        new_params[:, cols] = params[:, cols] - 0.7 * (clipped + 0.9 * fresh)


def per_device(pseudo_grad, params, momentum):
    groups = lax.axis_size("replica")
    devices = groups * lax.axis_size("fsdp")
    rows, columns = params.shape
    width = columns // groups
    count = rows * lax.axis_size("fsdp") * columns
    limit = pltpu.CompilerParams(vmem_limit_bytes=LIMIT)
    piece = jax.ShapeDtypeStruct((rows, width), pseudo_grad.dtype)
    pieces = pl.pallas_call(
        cut_kernel,
        out_shape=[piece] * groups,
        in_specs=[HBM],
        out_specs=[VMEM] * groups,
        scratch_shapes=[pltpu.SemaphoreType.DMA((groups,))],
        compiler_params=limit,
    )(pseudo_grad)
    order = [k for k in range(1, groups) if k > 1] + [1]
    moved = {0: pieces[0]}
    for k in order:
        moved[k] = swapped(pieces[k], "replica", k)
    average, squares = pl.pallas_call(
        average_kernel,
        out_shape=[
            jax.ShapeDtypeStruct((rows, width), WIDE),
            jax.ShapeDtypeStruct((devices, 1, 128), WIDE),
        ],
        in_specs=[VMEM] * groups,
        out_specs=[VMEM] * 2,
        compiler_params=limit,
    )(*[moved[k] for k in range(groups)])
    averages = {0: average}
    for k in range(2, groups, 2):
        averages[k] = swapped(average, "replica", k)
    averages[1] = swapped(average, "replica", 1)
    squares = lax.all_to_all(
        squares, ("replica", "fsdp"), split_axis=0, concat_axis=0, tiled=True
    )
    squares, averages = lax.optimization_barrier((squares, averages))
    for k in range(2, groups, 2):
        averages[k + 1] = swapped(averages[k], "replica", 1)
    out = jax.ShapeDtypeStruct((rows, columns), WIDE)
    return pl.pallas_call(
        functools.partial(update_kernel, count),
        out_shape=[out, out],
        in_specs=[VMEM] * (3 + groups),
        out_specs=[VMEM] * 2,
        compiler_params=limit,
    )(squares, params, momentum, *[averages[k] for k in range(groups)])


def solution(mesh):
    placed = (P("replica", "fsdp", None), P("fsdp", None), P("fsdp", None))
    return jax.shard_map(
        per_device,
        mesh=mesh,
        in_specs=placed,
        out_specs=(P("fsdp", None), P("fsdp", None)),
        check_vma=False,
    )
```

```python
import functools

import jax
import jax.numpy as jnp
from jax import lax
from jax.experimental import pallas as pl
from jax.experimental.pallas import tpu as pltpu
from jax.sharding import PartitionSpec as P

WIDE = jnp.float32
VMEM = pl.BlockSpec(memory_space=pltpu.VMEM)
HBM = pl.BlockSpec(memory_space=pltpu.HBM)
LIMIT = 16 * 1024 * 1024


def swapped(value, axis, flip):
    size = lax.axis_size(axis)
    return lax.ppermute(value, axis, [(i, i ^ flip) for i in range(size)])


def piece_of(k, width):
    return pl.ds(pl.multiple_of((lax.axis_index("replica") ^ k) * width, width), width)


def tree(parts):
    while len(parts) > 1:
        parts = [parts[i] + parts[i + 1] for i in range(0, len(parts), 2)]
    return parts[0]


def cut_kernel(grad, *rest):
    pieces, sems = rest[:-1], rest[-1]
    width = pieces[0].shape[1]
    copies = [
        pltpu.make_async_copy(grad.at[0, :, piece_of(k, width)], piece, sems.at[k])
        for k, piece in enumerate(pieces)
    ]
    for copy in copies:
        copy.start()
    for copy in copies:
        copy.wait()


def average_kernel(*refs):
    pieces, (average, squares) = refs[:-2], refs[-2:]
    total = tree([piece[...].astype(WIDE) for piece in pieces])
    mean = total / WIDE(len(pieces))
    average[...] = mean
    row = jnp.sum(mean * mean, axis=0, keepdims=True)
    lanes = functools.reduce(
        jnp.add, [row[:, i : i + 128] for i in range(0, row.shape[1], 128)]
    )
    squares[...] = jnp.broadcast_to(lanes[None], squares.shape)


def fetch_kernel(*refs):
    half = (len(refs) - 1) // 2
    copies = [
        pltpu.make_async_copy(refs[i], refs[half + i], refs[-1].at[i])
        for i in range(half)
    ]
    for copy in copies:
        copy.start()
    for copy in copies:
        copy.wait()


def update_kernel(count, flips, passed, squares, params, momentum, *refs):
    averages, refs = refs[: len(flips)], refs[len(flips) + passed :]
    new_params, new_momentum, params_out, momentum_out, sems = refs
    square_sum = jnp.sum(squares[...], keepdims=True).reshape(1, 1)
    factor = 0.2 / jnp.sqrt(square_sum / WIDE(count) + 1e-06)
    width = averages[0].shape[1]
    copies = []
    for i, (k, average) in enumerate(zip(flips, averages)):
        cols = piece_of(k, width)
        clipped = factor * average[...]
        fresh = 0.9 * momentum[:, cols] + clipped
        momentum_out[i] = fresh
        params_out[i] = params[:, cols] - 0.7 * (clipped + 0.9 * fresh)
        copies += [
            pltpu.make_async_copy(momentum_out.at[i], new_momentum.at[:, cols], sems.at[0, i]),
            pltpu.make_async_copy(params_out.at[i], new_params.at[:, cols], sems.at[1, i]),
        ]
        copies[-2].start()
        copies[-1].start()
    for copy in copies:
        copy.wait()


def update(count, flips, averages, squares, params, momentum, earlier=()):
    rows, width = averages[0].shape
    out = jax.ShapeDtypeStruct(params.shape, WIDE)
    first = 3 + len(flips)
    return pl.pallas_call(
        functools.partial(update_kernel, count, flips, len(earlier)),
        out_shape=[out, out],
        in_specs=[VMEM] * first + [HBM] * len(earlier),
        out_specs=[HBM] * 2,
        scratch_shapes=[
            pltpu.VMEM((len(flips), rows, width), WIDE),
            pltpu.VMEM((len(flips), rows, width), WIDE),
            pltpu.SemaphoreType.DMA((2, len(flips))),
        ],
        input_output_aliases={first + i: i for i in range(len(earlier))},
        compiler_params=pltpu.CompilerParams(vmem_limit_bytes=LIMIT),
    )(squares, params, momentum, *averages, *earlier)


def per_device(pseudo_grad, params, momentum):
    groups = lax.axis_size("replica")
    devices = groups * lax.axis_size("fsdp")
    rows, columns = params.shape
    width = columns // groups
    count = rows * lax.axis_size("fsdp") * columns
    limit = pltpu.CompilerParams(vmem_limit_bytes=LIMIT)
    piece = jax.ShapeDtypeStruct((rows, width), pseudo_grad.dtype)
    pieces = pl.pallas_call(
        cut_kernel,
        out_shape=[piece] * groups,
        in_specs=[HBM],
        out_specs=[VMEM] * groups,
        scratch_shapes=[pltpu.SemaphoreType.DMA((groups,))],
        compiler_params=limit,
    )(pseudo_grad)
    pieces, params, momentum = lax.optimization_barrier((pieces, params, momentum))
    kept = jax.ShapeDtypeStruct(params.shape, WIDE)
    params, momentum = pl.pallas_call(
        fetch_kernel,
        out_shape=[kept, kept],
        in_specs=[HBM] * 2,
        out_specs=[VMEM] * 2,
        scratch_shapes=[pltpu.SemaphoreType.DMA((2,))],
        compiler_params=limit,
        cost_estimate=pl.CostEstimate(flops=0, bytes_accessed=8 * params.size, transcendentals=0),
    )(params, momentum)
    moved = {k: swapped(pieces[k], "replica", k) for k in range(2, groups)}
    near, params, momentum = lax.optimization_barrier((pieces[1], params, momentum))
    moved.update({0: pieces[0], 1: swapped(near, "replica", 1)})
    average, squares = pl.pallas_call(
        average_kernel,
        out_shape=[
            jax.ShapeDtypeStruct((rows, width), WIDE),
            jax.ShapeDtypeStruct((devices, 1, 128), WIDE),
        ],
        in_specs=[VMEM] * groups,
        out_specs=[VMEM] * 2,
        compiler_params=limit,
    )(*[moved[k] for k in range(groups)])
    averages = {0: average}
    for k in range(2, groups, 2):
        averages[k] = swapped(average, "replica", k)
    averages[1] = swapped(average, "replica", 1)
    squares = lax.all_to_all(
        squares, ("replica", "fsdp"), split_axis=0, concat_axis=0, tiled=True
    )
    squares, averages = lax.optimization_barrier((squares, averages))
    for k in range(2, groups, 2):
        averages[k + 1] = swapped(averages[k], "replica", 1)
    here = [k for k in range(groups) if k < 2 or k % 2 == 0]
    late = [k for k in range(groups) if k not in here]
    outs = update(count, here, [averages[k] for k in here], squares, params, momentum)
    if late:
        outs = update(
            count, late, [averages[k] for k in late], squares, params, momentum, outs
        )
    return outs


def solution(mesh):
    placed = (P("replica", "fsdp", None), P("fsdp", None), P("fsdp", None))
    return jax.shard_map(
        per_device,
        mesh=mesh,
        in_specs=placed,
        out_specs=(P("fsdp", None), P("fsdp", None)),
        check_vma=False,
    )
```

```python
import functools

import jax
import jax.numpy as jnp
from jax import lax
from jax.experimental import pallas as pl
from jax.experimental.pallas import tpu as pltpu
from jax.sharding import PartitionSpec as P

WIDE = jnp.float32
VMEM = pl.BlockSpec(memory_space=pltpu.VMEM)
HBM = pl.BlockSpec(memory_space=pltpu.HBM)
LIMIT = 16 * 1024 * 1024


def swapped(value, axis, flip):
    size = lax.axis_size(axis)
    return lax.ppermute(value, axis, [(i, i ^ flip) for i in range(size)])


def piece_of(k, width):
    return pl.ds(pl.multiple_of((lax.axis_index("replica") ^ k) * width, width), width)


def tree(parts):
    while len(parts) > 1:
        parts = [parts[i] + parts[i + 1] for i in range(0, len(parts), 2)]
    return parts[0]


def cut_kernel(grad, *rest):
    pieces, sems = rest[:-1], rest[-1]
    width = pieces[0].shape[1]
    copies = [
        pltpu.make_async_copy(grad.at[0, :, piece_of(k, width)], piece, sems.at[k])
        for k, piece in enumerate(pieces)
    ]
    for copy in copies:
        copy.start()
    for copy in copies:
        copy.wait()


def average_kernel(*refs):
    pieces, (average, squares) = refs[:-2], refs[-2:]
    total = tree([piece[...].astype(WIDE) for piece in pieces])
    mean = total / WIDE(len(pieces))
    average[...] = mean
    row = jnp.sum(mean * mean, axis=0, keepdims=True)
    lanes = functools.reduce(
        jnp.add, [row[:, i : i + 128] for i in range(0, row.shape[1], 128)]
    )
    squares[...] = lanes


def add_kernel(left, right, out):
    out[...] = left[...] + right[...]


def fetch_kernel(*refs):
    half = (len(refs) - 1) // 2
    copies = [
        pltpu.make_async_copy(refs[i], refs[half + i], refs[-1].at[i])
        for i in range(half)
    ]
    for copy in copies:
        copy.start()
    for copy in copies:
        copy.wait()


def update_kernel(count, flips, near, far, params, momentum, *refs):
    averages, refs = refs[: len(flips)], refs[len(flips) :]
    new_params, new_momentum, params_out, momentum_out, sems = refs
    square_sum = jnp.sum(near[...] + far[...], axis=1, keepdims=True)
    factor = 0.2 / jnp.sqrt(square_sum / WIDE(count) + 1e-06)
    width = averages[0].shape[1]
    copies = []
    for i, (k, average) in enumerate(zip(flips, averages)):
        cols = piece_of(k, width)
        clipped = factor * average[...]
        fresh = 0.9 * momentum[:, cols] + clipped
        momentum_out[i] = fresh
        params_out[i] = params[:, cols] - 0.7 * (clipped + 0.9 * fresh)
        copies += [
            pltpu.make_async_copy(momentum_out.at[i], new_momentum.at[:, cols], sems.at[0, i]),
            pltpu.make_async_copy(params_out.at[i], new_params.at[:, cols], sems.at[1, i]),
        ]
        copies[-2].start()
        copies[-1].start()
    for copy in copies:
        copy.wait()


def update(count, averages, near, far, params, momentum):
    flips = sorted(averages)
    rows, width = averages[0].shape
    out = jax.ShapeDtypeStruct(params.shape, WIDE)
    return pl.pallas_call(
        functools.partial(update_kernel, count, flips),
        out_shape=[out, out],
        in_specs=[VMEM] * (4 + len(flips)),
        out_specs=[HBM] * 2,
        scratch_shapes=[
            pltpu.VMEM((len(flips), rows, width), WIDE),
            pltpu.VMEM((len(flips), rows, width), WIDE),
            pltpu.SemaphoreType.DMA((2, len(flips))),
        ],
        compiler_params=pltpu.CompilerParams(vmem_limit_bytes=LIMIT),
    )(near, far, params, momentum, *[averages[k] for k in flips])


def add(left, right):
    return pl.pallas_call(
        add_kernel,
        out_shape=jax.ShapeDtypeStruct(left.shape, left.dtype),
        in_specs=[VMEM] * 2,
        out_specs=VMEM,
        compiler_params=pltpu.CompilerParams(vmem_limit_bytes=LIMIT),
    )(left, right)


def per_device(pseudo_grad, params, momentum):
    groups = lax.axis_size("replica")
    rows, columns = params.shape
    width = columns // groups
    count = rows * lax.axis_size("fsdp") * columns
    limit = pltpu.CompilerParams(vmem_limit_bytes=LIMIT)
    piece = jax.ShapeDtypeStruct((rows, width), pseudo_grad.dtype)
    pieces = pl.pallas_call(
        cut_kernel,
        out_shape=[piece] * groups,
        in_specs=[HBM],
        out_specs=[VMEM] * groups,
        scratch_shapes=[pltpu.SemaphoreType.DMA((groups,))],
        compiler_params=limit,
    )(pseudo_grad)
    pieces, params, momentum = lax.optimization_barrier((pieces, params, momentum))
    kept = jax.ShapeDtypeStruct(params.shape, WIDE)
    params, momentum = pl.pallas_call(
        fetch_kernel,
        out_shape=[kept, kept],
        in_specs=[HBM] * 2,
        out_specs=[VMEM] * 2,
        scratch_shapes=[pltpu.SemaphoreType.DMA((2,))],
        compiler_params=limit,
        cost_estimate=pl.CostEstimate(flops=0, bytes_accessed=8 * params.size, transcendentals=0),
    )(params, momentum)
    moved = {k: swapped(pieces[k], "replica", k) for k in range(2, groups)}
    near, params, momentum = lax.optimization_barrier((pieces[1], params, momentum))
    moved.update({0: pieces[0], 1: swapped(near, "replica", 1)})
    average, squares = pl.pallas_call(
        average_kernel,
        out_shape=[
            jax.ShapeDtypeStruct((rows, width), WIDE),
            jax.ShapeDtypeStruct((1, 128), WIDE),
        ],
        in_specs=[VMEM] * groups,
        out_specs=[VMEM] * 2,
        compiler_params=limit,
    )(*[moved[k] for k in range(groups)])
    averages = {0: average}
    for k in range(2, groups, 2):
        averages[k] = swapped(average, "replica", k)
    near, far = squares, jnp.zeros_like(squares)
    steps = [
        (axis, 1 << i)
        for axis in ("fsdp", "replica")
        for i in range((lax.axis_size(axis) - 1).bit_length())
    ]
    for i, (axis, flip) in enumerate(steps):
        if i:
            near = add(near, far)
        if i == 1:
            near, average = lax.optimization_barrier((near, average))
            averages[1] = swapped(average, "replica", 1)
        if i == len(steps) - 1:
            near, averages = lax.optimization_barrier((near, averages))
        far = swapped(near, axis, flip)
    for k in range(2, groups, 2):
        averages[k + 1] = swapped(averages[k], "replica", 1)
    return update(count, averages, near, far, params, momentum)


def solution(mesh):
    placed = (P("replica", "fsdp", None), P("fsdp", None), P("fsdp", None))
    return jax.shard_map(
        per_device,
        mesh=mesh,
        in_specs=placed,
        out_specs=(P("fsdp", None), P("fsdp", None)),
        check_vma=False,
    )
```

```python
import functools

import jax
import jax.numpy as jnp
from jax import lax
from jax.experimental import pallas as pl
from jax.experimental.pallas import tpu as pltpu
from jax.sharding import PartitionSpec as P

WIDE = jnp.float32
VMEM = pl.BlockSpec(memory_space=pltpu.VMEM)
HBM = pl.BlockSpec(memory_space=pltpu.HBM)
LIMIT = 16 * 1024 * 1024


def swapped(value, axis, flip):
    size = lax.axis_size(axis)
    return lax.ppermute(value, axis, [(i, i ^ flip) for i in range(size)])


def piece_of(k, width):
    return pl.ds(pl.multiple_of((lax.axis_index("replica") ^ k) * width, width), width)


def tree(parts):
    while len(parts) > 1:
        parts = [parts[i] + parts[i + 1] for i in range(0, len(parts), 2)]
    return parts[0]


def cut_kernel(grad, *rest):
    pieces, sems = rest[:-1], rest[-1]
    width = pieces[0].shape[1]
    copies = [
        pltpu.make_async_copy(grad.at[0, :, piece_of(k, width)], piece, sems.at[k])
        for k, piece in enumerate(pieces)
    ]
    for copy in copies:
        copy.start()
    for copy in copies:
        copy.wait()


def pair_kernel(own, own_mate, other, other_mate, own_sum, other_sum):
    own_sum[...] = own[...].astype(WIDE) + own_mate[...].astype(WIDE)
    other_sum[...] = other[...].astype(WIDE) + other_mate[...].astype(WIDE)


def average_kernel(groups, *refs):
    own, pieces, (average, squares) = refs[0], refs[1:-2], refs[-2:]
    pairs = [own[...]]
    for i in range(0, len(pieces), 2):
        pairs.append(pieces[i][...].astype(WIDE) + pieces[i + 1][...].astype(WIDE))
    mean = tree(pairs) / WIDE(groups)
    average[...] = mean
    row = jnp.sum(mean * mean, axis=0, keepdims=True)
    lanes = functools.reduce(
        jnp.add, [row[:, i : i + 128] for i in range(0, row.shape[1], 128)]
    )
    squares[...] = jnp.broadcast_to(lanes[None], squares.shape)


def join_kernel(groups, here, there, average):
    average[...] = (here[...] + there[...]) / WIDE(groups)


def fetch_kernel(*refs):
    half = (len(refs) - 1) // 2
    copies = [
        pltpu.make_async_copy(refs[i], refs[half + i], refs[-1].at[i])
        for i in range(half)
    ]
    for copy in copies:
        copy.start()
    for copy in copies:
        copy.wait()


def update_kernel(count, flips, passed, squares, params, momentum, *refs):
    averages, refs = refs[: len(flips)], refs[len(flips) + passed :]
    new_params, new_momentum, params_out, momentum_out, sems = refs
    square_sum = jnp.sum(squares[...], keepdims=True).reshape(1, 1)
    factor = 0.2 / jnp.sqrt(square_sum / WIDE(count) + 1e-06)
    width = averages[0].shape[1]
    copies = []
    for i, (k, average) in enumerate(zip(flips, averages)):
        cols = piece_of(k, width)
        clipped = factor * average[...]
        fresh = 0.9 * momentum[:, cols] + clipped
        momentum_out[i] = fresh
        params_out[i] = params[:, cols] - 0.7 * (clipped + 0.9 * fresh)
        copies += [
            pltpu.make_async_copy(momentum_out.at[i], new_momentum.at[:, cols], sems.at[0, i]),
            pltpu.make_async_copy(params_out.at[i], new_params.at[:, cols], sems.at[1, i]),
        ]
        copies[-2].start()
        copies[-1].start()
    for copy in copies:
        copy.wait()


def update(count, flips, averages, squares, params, momentum, earlier=()):
    rows, width = averages[0].shape
    out = jax.ShapeDtypeStruct(params.shape, WIDE)
    first = 3 + len(flips)
    return pl.pallas_call(
        functools.partial(update_kernel, count, flips, len(earlier)),
        out_shape=[out, out],
        in_specs=[VMEM] * first + [HBM] * len(earlier),
        out_specs=[HBM] * 2,
        scratch_shapes=[
            pltpu.VMEM((len(flips), rows, width), WIDE),
            pltpu.VMEM((len(flips), rows, width), WIDE),
            pltpu.SemaphoreType.DMA((2, len(flips))),
        ],
        input_output_aliases={first + i: i for i in range(len(earlier))},
        compiler_params=pltpu.CompilerParams(vmem_limit_bytes=LIMIT),
    )(squares, params, momentum, *averages, *earlier)


def call(kernel, out_shape, *args, scratch=()):
    return pl.pallas_call(
        kernel,
        out_shape=out_shape,
        in_specs=[VMEM] * len(args),
        out_specs=jax.tree.map(lambda _: VMEM, out_shape),
        scratch_shapes=scratch,
        compiler_params=pltpu.CompilerParams(vmem_limit_bytes=LIMIT),
    )(*args)


def per_device(pseudo_grad, params, momentum):
    groups = lax.axis_size("replica")
    devices = groups * lax.axis_size("fsdp")
    rows, columns = params.shape
    width = columns // groups
    count = rows * lax.axis_size("fsdp") * columns
    piece = jax.ShapeDtypeStruct((rows, width), pseudo_grad.dtype)
    wide_piece = jax.ShapeDtypeStruct((rows, width), WIDE)
    others = range(2, groups, 2)

    pieces = call(
        cut_kernel, [piece] * groups, pseudo_grad,
        scratch=[pltpu.SemaphoreType.DMA((groups,))],
    )
    direct = {k: swapped(pieces[k], "replica", k) for k in others}
    near = {k: swapped(pieces[k + 1], "replica", 1) for k in others}
    near, last = lax.optimization_barrier((near, pieces[1]))
    relayed = {k: swapped(near[k], "replica", k) for k in others}
    direct, momentum = lax.optimization_barrier((direct, momentum))
    mate = swapped(last, "replica", 1)
    (momentum,) = call(
        fetch_kernel, [jax.ShapeDtypeStruct(params.shape, WIDE)], momentum,
        scratch=[pltpu.SemaphoreType.DMA((1,))],
    )
    own_sum, other_sum = call(
        pair_kernel, [wide_piece] * 2,
        pieces[0], mate, pieces[2 % groups], near.get(2, mate),
    )
    averages = {}
    if groups == 4:
        own_sum, momentum = lax.optimization_barrier((own_sum, momentum))
        across = swapped(own_sum, "replica", 2)
    averages[0], squares = call(
        functools.partial(average_kernel, groups),
        [wide_piece, jax.ShapeDtypeStruct((devices, 1, 128), WIDE)],
        own_sum, *[x[k] for k in others for x in (direct, relayed)],
    )
    averages[1] = swapped(averages[0], "replica", 1)
    if groups != 4:
        averages.update({k: swapped(averages[0], "replica", k) for k in others})
    squares = lax.all_to_all(
        squares, ("replica", "fsdp"), split_axis=0, concat_axis=0, tiled=True
    )
    if groups == 4:
        squares, across = lax.optimization_barrier((squares, across))
        averages[2] = call(
            functools.partial(join_kernel, groups), wide_piece, other_sum, across
        )
    squares, averages = lax.optimization_barrier((squares, averages))
    for k in others:
        averages[k + 1] = swapped(averages[k], "replica", 1)
    here = [k for k in range(groups) if k < 2 or k % 2 == 0]
    late = [k for k in range(groups) if k not in here]
    outs = update(count, here, [averages[k] for k in here], squares, params, momentum)
    if late:
        outs = update(
            count, late, [averages[k] for k in late], squares, params, momentum, outs
        )
    return outs


def solution(mesh):
    placed = (P("replica", "fsdp", None), P("fsdp", None), P("fsdp", None))
    return jax.shard_map(
        per_device,
        mesh=mesh,
        in_specs=placed,
        out_specs=(P("fsdp", None), P("fsdp", None)),
        check_vma=False,
    )
```

```python
import functools

import jax
import jax.numpy as jnp
from jax import lax
from jax.experimental import pallas as pl
from jax.experimental.pallas import tpu as pltpu
from jax.sharding import PartitionSpec as P

WIDE = jnp.float32
VMEM = pl.BlockSpec(memory_space=pltpu.VMEM)
HBM = pl.BlockSpec(memory_space=pltpu.HBM)
LIMIT = 16 * 1024 * 1024


def swapped(value, axis, flip):
    size = lax.axis_size(axis)
    return lax.ppermute(value, axis, [(i, i ^ flip) for i in range(size)])


def piece_of(k, width):
    return pl.ds(pl.multiple_of((lax.axis_index("replica") ^ k) * width, width), width)


def tree(parts):
    while len(parts) > 1:
        parts = [parts[i] + parts[i + 1] for i in range(0, len(parts), 2)]
    return parts[0]


def cut_kernel(grad, *rest):
    pieces, sems = rest[:-1], rest[-1]
    width = pieces[0].shape[1]
    copies = [
        pltpu.make_async_copy(grad.at[0, :, piece_of(k, width)], piece, sems.at[k])
        for k, piece in enumerate(pieces)
    ]
    for copy in copies:
        copy.start()
    for copy in copies:
        copy.wait()


def average_kernel(*refs):
    pieces, (average, squares) = refs[:-2], refs[-2:]
    total = tree([piece[...].astype(WIDE) for piece in pieces])
    mean = total / WIDE(len(pieces))
    average[...] = mean
    row = jnp.sum(mean * mean, axis=0, keepdims=True)
    lanes = functools.reduce(
        jnp.add, [row[:, i : i + 128] for i in range(0, row.shape[1], 128)]
    )
    squares[...] = jnp.broadcast_to(lanes[None], squares.shape)


def fetch_kernel(*refs):
    half = (len(refs) - 1) // 2
    copies = [
        pltpu.make_async_copy(refs[i], refs[half + i], refs[-1].at[i])
        for i in range(half)
    ]
    for copy in copies:
        copy.start()
    for copy in copies:
        copy.wait()


def update_kernel(count, flips, passed, squares, params, momentum, *refs):
    averages, refs = refs[: len(flips)], refs[len(flips) + passed :]
    new_params, new_momentum, params_out, momentum_out, sems = refs
    square_sum = jnp.sum(squares[...], keepdims=True).reshape(1, 1)
    factor = 0.2 / jnp.sqrt(square_sum / WIDE(count) + 1e-06)
    width = averages[0].shape[1]
    copies = []
    for i, (k, average) in enumerate(zip(flips, averages)):
        cols = piece_of(k, width)
        clipped = factor * average[...]
        fresh = 0.9 * momentum[:, cols] + clipped
        momentum_out[i] = fresh
        params_out[i] = params[:, cols] - 0.7 * (clipped + 0.9 * fresh)
        copies += [
            pltpu.make_async_copy(momentum_out.at[i], new_momentum.at[:, cols], sems.at[0, i]),
            pltpu.make_async_copy(params_out.at[i], new_params.at[:, cols], sems.at[1, i]),
        ]
        copies[-2].start()
        copies[-1].start()
    for copy in copies:
        copy.wait()


def update(count, flips, averages, squares, params, momentum, earlier=()):
    rows, width = averages[0].shape
    out = jax.ShapeDtypeStruct(params.shape, WIDE)
    first = 3 + len(flips)
    return pl.pallas_call(
        functools.partial(update_kernel, count, flips, len(earlier)),
        out_shape=[out, out],
        in_specs=[VMEM] * first + [HBM] * len(earlier),
        out_specs=[HBM] * 2,
        scratch_shapes=[
            pltpu.VMEM((len(flips), rows, width), WIDE),
            pltpu.VMEM((len(flips), rows, width), WIDE),
            pltpu.SemaphoreType.DMA((2, len(flips))),
        ],
        input_output_aliases={first + i: i for i in range(len(earlier))},
        compiler_params=pltpu.CompilerParams(vmem_limit_bytes=LIMIT),
    )(squares, params, momentum, *averages, *earlier)


def per_device(pseudo_grad, params, momentum):
    groups = lax.axis_size("replica")
    devices = groups * lax.axis_size("fsdp")
    rows, columns = params.shape
    width = columns // groups
    count = rows * lax.axis_size("fsdp") * columns
    limit = pltpu.CompilerParams(vmem_limit_bytes=LIMIT)
    piece = jax.ShapeDtypeStruct((rows, width), pseudo_grad.dtype)
    pieces = pl.pallas_call(
        cut_kernel,
        out_shape=[piece] * groups,
        in_specs=[HBM],
        out_specs=[VMEM] * groups,
        scratch_shapes=[pltpu.SemaphoreType.DMA((groups,))],
        compiler_params=limit,
    )(pseudo_grad)
    pieces, params, momentum = lax.optimization_barrier((pieces, params, momentum))
    kept = jax.ShapeDtypeStruct(params.shape, WIDE)
    params, momentum = pl.pallas_call(
        fetch_kernel,
        out_shape=[kept, kept],
        in_specs=[HBM] * 2,
        out_specs=[VMEM] * 2,
        scratch_shapes=[pltpu.SemaphoreType.DMA((2,))],
        compiler_params=limit,
        cost_estimate=pl.CostEstimate(flops=0, bytes_accessed=8 * params.size, transcendentals=0),
    )(params, momentum)
    moved = {k: swapped(pieces[k], "replica", k) for k in range(2, groups)}
    near, params, momentum = lax.optimization_barrier((pieces[1], params, momentum))
    moved.update({0: pieces[0], 1: swapped(near, "replica", 1)})
    average, squares = pl.pallas_call(
        average_kernel,
        out_shape=[
            jax.ShapeDtypeStruct((rows, width), WIDE),
            jax.ShapeDtypeStruct((devices, 1, 128), WIDE),
        ],
        in_specs=[VMEM] * groups,
        out_specs=[VMEM] * 2,
        compiler_params=limit,
    )(*[moved[k] for k in range(groups)])
    averages = {0: average}
    for k in range(2, groups, 2):
        averages[k] = swapped(average, "replica", k)
    averages[1] = swapped(average, "replica", 1)
    squares = lax.all_to_all(
        squares, ("fsdp", "replica"), split_axis=0, concat_axis=0, tiled=True
    )
    squares, averages = lax.optimization_barrier((squares, averages))
    for k in range(2, groups, 2):
        averages[k + 1] = swapped(averages[k], "replica", 1)
    here = [k for k in range(groups) if k < 2 or k % 2 == 0]
    late = [k for k in range(groups) if k not in here]
    outs = update(count, here, [averages[k] for k in here], squares, params, momentum)
    if late:
        outs = update(
            count, late, [averages[k] for k in late], squares, params, momentum, outs
        )
    return outs


def solution(mesh):
    placed = (P("replica", "fsdp", None), P("fsdp", None), P("fsdp", None))
    return jax.shard_map(
        per_device,
        mesh=mesh,
        in_specs=placed,
        out_specs=(P("fsdp", None), P("fsdp", None)),
        check_vma=False,
    )
```

```python
import functools

import jax
import jax.numpy as jnp
from jax import lax
from jax.experimental import pallas as pl
from jax.experimental.pallas import tpu as pltpu
from jax.sharding import PartitionSpec as P

WIDE = jnp.float32
VMEM = pl.BlockSpec(memory_space=pltpu.VMEM)
HBM = pl.BlockSpec(memory_space=pltpu.HBM)
LIMIT = 16 * 1024 * 1024
LINE = 2


def swapped(value, axis, flip):
    size = lax.axis_size(axis)
    return lax.ppermute(value, axis, [(i, i ^ flip) for i in range(size)])


def piece_of(k, width):
    return pl.ds(pl.multiple_of((lax.axis_index("replica") ^ k) * width, width), width)


def tree(parts):
    while len(parts) > 1:
        parts = [functools.reduce(jnp.add, parts[i : i + 2]) for i in range(0, len(parts), 2)]
    return parts[0]


def cut_kernel(grad, *rest):
    pieces, sems = rest[:-1], rest[-1]
    width = pieces[0].shape[1]
    copies = [
        pltpu.make_async_copy(grad.at[0, :, piece_of(k, width)], piece, sems.at[k])
        for k, piece in enumerate(pieces)
    ]
    for copy in copies:
        copy.start()
    for copy in copies:
        copy.wait()


def average_kernel(*refs):
    pieces, (average, squares) = refs[:-2], refs[-2:]
    total = tree([piece[...].astype(WIDE) for piece in pieces])
    mean = total / WIDE(len(pieces))
    average[...] = mean
    row = jnp.sum(mean * mean, axis=0, keepdims=True)
    lanes = functools.reduce(
        jnp.add, [row[:, i : i + 128] for i in range(0, row.shape[1], 128)]
    )
    squares[...] = lanes


def add_kernel(*refs):
    refs[-1][...] = tree([ref[...] for ref in refs[:-1]])


def pick_kernel(own, *refs):
    first = lax.axis_index("fsdp") < LINE
    refs[-1][...] = jnp.where(first, own[...], functools.reduce(jnp.add, [ref[...] for ref in refs[:-1]]))


def fetch_kernel(*refs):
    half = (len(refs) - 1) // 2
    copies = [
        pltpu.make_async_copy(refs[i], refs[half + i], refs[-1].at[i])
        for i in range(half)
    ]
    for copy in copies:
        copy.start()
    for copy in copies:
        copy.wait()


def update_kernel(count, flips, near, far, params, momentum, *refs):
    averages, refs = refs[: len(flips)], refs[len(flips) :]
    new_params, new_momentum, params_out, momentum_out, sems = refs
    square_sum = jnp.sum(near[...] + far[...], axis=1, keepdims=True)
    factor = 0.2 / jnp.sqrt(square_sum / WIDE(count) + 1e-06)
    width = averages[0].shape[1]
    copies = []
    for i, (k, average) in enumerate(zip(flips, averages)):
        cols = piece_of(k, width)
        clipped = factor * average[...]
        fresh = 0.9 * momentum[:, cols] + clipped
        momentum_out[i] = fresh
        params_out[i] = params[:, cols] - 0.7 * (clipped + 0.9 * fresh)
        copies += [
            pltpu.make_async_copy(momentum_out.at[i], new_momentum.at[:, cols], sems.at[0, i]),
            pltpu.make_async_copy(params_out.at[i], new_params.at[:, cols], sems.at[1, i]),
        ]
        copies[-2].start()
        copies[-1].start()
    for copy in copies:
        copy.wait()


def update(count, averages, near, far, params, momentum):
    flips = sorted(averages)
    rows, width = averages[0].shape
    out = jax.ShapeDtypeStruct(params.shape, WIDE)
    return pl.pallas_call(
        functools.partial(update_kernel, count, flips),
        out_shape=[out, out],
        in_specs=[VMEM] * (4 + len(flips)),
        out_specs=[HBM] * 2,
        scratch_shapes=[
            pltpu.VMEM((len(flips), rows, width), WIDE),
            pltpu.VMEM((len(flips), rows, width), WIDE),
            pltpu.SemaphoreType.DMA((2, len(flips))),
        ],
        compiler_params=pltpu.CompilerParams(vmem_limit_bytes=LIMIT),
    )(near, far, params, momentum, *[averages[k] for k in flips])


def small(kernel, *args):
    return pl.pallas_call(
        kernel,
        out_shape=jax.ShapeDtypeStruct(args[0].shape, args[0].dtype),
        in_specs=[VMEM] * len(args),
        out_specs=VMEM,
        compiler_params=pltpu.CompilerParams(vmem_limit_bytes=LIMIT),
    )(*args)


def line_sends(value, back):
    size = lax.axis_size("fsdp")
    moves = [[(f + m, f) for f in range(LINE)] for m in range(LINE, size, LINE)]
    moves.reverse()
    return [
        lax.ppermute(value, "fsdp", [(b, a) if back else (a, b) for a, b in move])
        for move in moves
    ]


def per_device(pseudo_grad, params, momentum):
    groups = lax.axis_size("replica")
    rows, columns = params.shape
    width = columns // groups
    count = rows * lax.axis_size("fsdp") * columns
    limit = pltpu.CompilerParams(vmem_limit_bytes=LIMIT)
    piece = jax.ShapeDtypeStruct((rows, width), pseudo_grad.dtype)
    pieces = pl.pallas_call(
        cut_kernel,
        out_shape=[piece] * groups,
        in_specs=[HBM],
        out_specs=[VMEM] * groups,
        scratch_shapes=[pltpu.SemaphoreType.DMA((groups,))],
        compiler_params=limit,
    )(pseudo_grad)
    pieces, params, momentum = lax.optimization_barrier((pieces, params, momentum))
    kept = jax.ShapeDtypeStruct(params.shape, WIDE)
    params, momentum = pl.pallas_call(
        fetch_kernel,
        out_shape=[kept, kept],
        in_specs=[HBM] * 2,
        out_specs=[VMEM] * 2,
        scratch_shapes=[pltpu.SemaphoreType.DMA((2,))],
        compiler_params=limit,
        cost_estimate=pl.CostEstimate(flops=0, bytes_accessed=8 * params.size, transcendentals=0),
    )(params, momentum)
    moved = {k: swapped(pieces[k], "replica", k) for k in range(2, groups)}
    near, params, momentum = lax.optimization_barrier((pieces[1], params, momentum))
    moved.update({0: pieces[0], 1: swapped(near, "replica", 1)})
    average, squares = pl.pallas_call(
        average_kernel,
        out_shape=[
            jax.ShapeDtypeStruct((rows, width), WIDE),
            jax.ShapeDtypeStruct((1, 128), WIDE),
        ],
        in_specs=[VMEM] * groups,
        out_specs=[VMEM] * 2,
        compiler_params=limit,
    )(*[moved[k] for k in range(groups)])
    parts = line_sends(squares, False)
    averages = {0: average, 1: swapped(average, "replica", 1)}
    for k in range(2, groups, 2):
        averages[k] = swapped(average, "replica", k)
    parts = [squares] + parts
    while len(parts) > 4:
        parts = [small(add_kernel, *parts[:4])] + parts[4:]
    total = small(add_kernel, *parts)
    near = small(pick_kernel, total, *line_sends(total, True))
    steps = [("fsdp", 1 << i) for i in range((LINE - 1).bit_length())]
    steps += [("replica", 1 << i) for i in range((groups - 1).bit_length())]
    far = None
    for i, (axis, flip) in enumerate(steps):
        if far is not None:
            near = small(add_kernel, near, far)
        if i == len(steps) - 1:
            near, averages = lax.optimization_barrier((near, averages))
        far = swapped(near, axis, flip)
    for k in range(2, groups, 2):
        averages[k + 1] = swapped(averages[k], "replica", 1)
    return update(count, averages, near, far, params, momentum)


def solution(mesh):
    placed = (P("replica", "fsdp", None), P("fsdp", None), P("fsdp", None))
    return jax.shard_map(
        per_device,
        mesh=mesh,
        in_specs=placed,
        out_specs=(P("fsdp", None), P("fsdp", None)),
        check_vma=False,
    )
```

```python
import functools

import jax
import jax.numpy as jnp
from jax import lax
from jax.experimental import pallas as pl
from jax.experimental.pallas import tpu as pltpu
from jax.sharding import PartitionSpec as P

WIDE = jnp.float32
VMEM = pl.BlockSpec(memory_space=pltpu.VMEM)
HBM = pl.BlockSpec(memory_space=pltpu.HBM)
LIMIT = 16 * 1024 * 1024


def swapped(value, axis, flip):
    size = lax.axis_size(axis)
    return lax.ppermute(value, axis, [(i, i ^ flip) for i in range(size)])


def piece_of(k, width):
    return pl.ds(pl.multiple_of((lax.axis_index("replica") ^ k) * width, width), width)


def tree(parts):
    while len(parts) > 1:
        parts = [parts[i] + parts[i + 1] for i in range(0, len(parts), 2)]
    return parts[0]


def cut_kernel(grad, *rest):
    pieces, sems = rest[:-1], rest[-1]
    width = pieces[0].shape[1]
    copies = [
        pltpu.make_async_copy(grad.at[0, :, piece_of(k, width)], piece, sems.at[k])
        for k, piece in enumerate(pieces)
    ]
    for copy in copies:
        copy.start()
    for copy in copies:
        copy.wait()


def pair_kernel(own, own_mate, other, other_mate, own_sum, other_sum):
    own_sum[...] = own[...].astype(WIDE) + own_mate[...].astype(WIDE)
    other_sum[...] = other[...].astype(WIDE) + other_mate[...].astype(WIDE)


def average_kernel(groups, *refs):
    own, pieces, (average, squares) = refs[0], refs[1:-2], refs[-2:]
    pairs = [own[...]]
    for i in range(0, len(pieces), 2):
        pairs.append(pieces[i][...].astype(WIDE) + pieces[i + 1][...].astype(WIDE))
    mean = tree(pairs) / WIDE(groups)
    average[...] = mean
    row = jnp.sum(mean * mean, axis=0, keepdims=True)
    lanes = functools.reduce(
        jnp.add, [row[:, i : i + 128] for i in range(0, row.shape[1], 128)]
    )
    squares[...] = jnp.broadcast_to(lanes[None], squares.shape)


def join_kernel(groups, here, there, there_mate, average):
    pair = there[...].astype(WIDE) + there_mate[...].astype(WIDE)
    average[...] = (here[...] + pair) / WIDE(groups)


def fetch_kernel(*refs):
    half = (len(refs) - 1) // 2
    copies = [
        pltpu.make_async_copy(refs[i], refs[half + i], refs[-1].at[i])
        for i in range(half)
    ]
    for copy in copies:
        copy.start()
    for copy in copies:
        copy.wait()


def update_kernel(count, flips, passed, squares, params, momentum, *refs):
    averages, refs = refs[: len(flips)], refs[len(flips) + passed :]
    new_params, new_momentum, params_out, momentum_out, sems = refs
    square_sum = jnp.sum(squares[...], keepdims=True).reshape(1, 1)
    factor = 0.2 / jnp.sqrt(square_sum / WIDE(count) + 1e-06)
    width = averages[0].shape[1]
    copies = []
    for i, (k, average) in enumerate(zip(flips, averages)):
        cols = piece_of(k, width)
        clipped = factor * average[...]
        fresh = 0.9 * momentum[:, cols] + clipped
        momentum_out[i] = fresh
        params_out[i] = params[:, cols] - 0.7 * (clipped + 0.9 * fresh)
        copies += [
            pltpu.make_async_copy(momentum_out.at[i], new_momentum.at[:, cols], sems.at[0, i]),
            pltpu.make_async_copy(params_out.at[i], new_params.at[:, cols], sems.at[1, i]),
        ]
        copies[-2].start()
        copies[-1].start()
    for copy in copies:
        copy.wait()


def update(count, flips, averages, squares, params, momentum, earlier=()):
    rows, width = averages[0].shape
    out = jax.ShapeDtypeStruct(params.shape, WIDE)
    first = 3 + len(flips)
    return pl.pallas_call(
        functools.partial(update_kernel, count, flips, len(earlier)),
        out_shape=[out, out],
        in_specs=[VMEM] * first + [HBM] * len(earlier),
        out_specs=[HBM] * 2,
        scratch_shapes=[
            pltpu.VMEM((len(flips), rows, width), WIDE),
            pltpu.VMEM((len(flips), rows, width), WIDE),
            pltpu.SemaphoreType.DMA((2, len(flips))),
        ],
        input_output_aliases={first + i: i for i in range(len(earlier))},
        compiler_params=pltpu.CompilerParams(vmem_limit_bytes=LIMIT),
    )(squares, params, momentum, *averages, *earlier)


def call(kernel, out_shape, *args, scratch=()):
    return pl.pallas_call(
        kernel,
        out_shape=out_shape,
        in_specs=[VMEM] * len(args),
        out_specs=jax.tree.map(lambda _: VMEM, out_shape),
        scratch_shapes=scratch,
        compiler_params=pltpu.CompilerParams(vmem_limit_bytes=LIMIT),
    )(*args)


def per_device(pseudo_grad, params, momentum):
    groups = lax.axis_size("replica")
    devices = groups * lax.axis_size("fsdp")
    rows, columns = params.shape
    width = columns // groups
    count = rows * lax.axis_size("fsdp") * columns
    piece = jax.ShapeDtypeStruct((rows, width), pseudo_grad.dtype)
    wide_piece = jax.ShapeDtypeStruct((rows, width), WIDE)
    others = range(2, groups, 2)

    pieces = call(
        cut_kernel, [piece] * groups, pseudo_grad,
        scratch=[pltpu.SemaphoreType.DMA((groups,))],
    )
    direct = {k: swapped(pieces[k], "replica", k) for k in range(2, groups)}
    (momentum,) = call(
        fetch_kernel, [jax.ShapeDtypeStruct(params.shape, WIDE)], momentum,
        scratch=[pltpu.SemaphoreType.DMA((1,))],
    )
    (zero, one, three), momentum = lax.optimization_barrier(
        ((pieces[0], pieces[1], pieces[3 % groups]), momentum)
    )
    mate = swapped(one, "replica", 1)
    mates_other = swapped(three, "replica", 1) if groups == 4 else mate
    own_sum, other_sum = call(
        pair_kernel, [wide_piece] * 2, pieces[0], mate, pieces[2 % groups], mates_other
    )
    averages = {}
    if groups == 4:
        zero, mate, direct[2] = lax.optimization_barrier((zero, mate, direct[2]))
        across = [swapped(x, "replica", 2) for x in (zero, mate)]
    averages[0], squares = call(
        functools.partial(average_kernel, groups),
        [wide_piece, jax.ShapeDtypeStruct((devices, 1, 128), WIDE)],
        own_sum, *[direct[k] for k in range(2, groups)],
    )
    if groups != 4:
        averages.update({k: swapped(averages[0], "replica", k) for k in others})
    squares = lax.all_to_all(
        squares, ("replica", "fsdp"), split_axis=0, concat_axis=0, tiled=True
    )
    if groups == 4:
        squares, across = lax.optimization_barrier((squares, across))
        averages[2] = call(
            functools.partial(join_kernel, groups), wide_piece, other_sum, *across
        )
    squares, averages = lax.optimization_barrier((squares, averages))
    here = range(0, groups, 2)
    late = range(1, groups, 2)
    for k in here:
        averages[k + 1] = swapped(averages[k], "replica", 1)
    outs = update(count, here, [averages[k] for k in here], squares, params, momentum)
    if late:
        outs = update(
            count, late, [averages[k] for k in late], squares, params, momentum, outs
        )
    return outs


def solution(mesh):
    placed = (P("replica", "fsdp", None), P("fsdp", None), P("fsdp", None))
    return jax.shard_map(
        per_device,
        mesh=mesh,
        in_specs=placed,
        out_specs=(P("fsdp", None), P("fsdp", None)),
        check_vma=False,
    )
```

```python
import functools

import jax
import jax.numpy as jnp
from jax import lax
from jax.experimental import pallas as pl
from jax.experimental.pallas import tpu as pltpu
from jax.sharding import PartitionSpec as P

WIDE = jnp.float32
VMEM = pl.BlockSpec(memory_space=pltpu.VMEM)
HBM = pl.BlockSpec(memory_space=pltpu.HBM)
LIMIT = 16 * 1024 * 1024


def swapped(value, axis, flip):
    size = lax.axis_size(axis)
    return lax.ppermute(value, axis, [(i, i ^ flip) for i in range(size)])


def piece_of(k, width):
    return pl.ds(pl.multiple_of((lax.axis_index("replica") ^ k) * width, width), width)


def tree(parts):
    while len(parts) > 1:
        parts = [parts[i] + parts[i + 1] for i in range(0, len(parts), 2)]
    return parts[0]


def cut_kernel(grad, *rest):
    pieces, sems = rest[:-1], rest[-1]
    width = pieces[0].shape[1]
    copies = [
        pltpu.make_async_copy(grad.at[0, :, piece_of(k, width)], piece, sems.at[k])
        for k, piece in enumerate(pieces)
    ]
    for copy in copies:
        copy.start()
    for copy in copies:
        copy.wait()


def average_kernel(*refs):
    pieces, (average, squares) = refs[:-2], refs[-2:]
    total = tree([piece[...].astype(WIDE) for piece in pieces])
    mean = total / WIDE(len(pieces))
    average[...] = mean
    row = jnp.sum(mean * mean, axis=0, keepdims=True)
    lanes = functools.reduce(
        jnp.add, [row[:, i : i + 128] for i in range(0, row.shape[1], 128)]
    )
    squares[...] = jnp.broadcast_to(lanes[None], squares.shape)


def fetch_kernel(*refs):
    half = (len(refs) - 1) // 2
    copies = [
        pltpu.make_async_copy(refs[i], refs[half + i], refs[-1].at[i])
        for i in range(half)
    ]
    for copy in copies:
        copy.start()
    for copy in copies:
        copy.wait()


def update_kernel(count, flips, passed, squares, params, momentum, *refs):
    averages, refs = refs[: len(flips)], refs[len(flips) + passed :]
    new_params, new_momentum, params_out, momentum_out, sems = refs
    square_sum = jnp.sum(squares[...], keepdims=True).reshape(1, 1)
    factor = 0.2 / jnp.sqrt(square_sum / WIDE(count) + 1e-06)
    width = averages[0].shape[1]
    copies = []
    for i, (k, average) in enumerate(zip(flips, averages)):
        cols = piece_of(k, width)
        clipped = factor * average[...]
        fresh = 0.9 * momentum[:, cols] + clipped
        momentum_out[i] = fresh
        params_out[i] = params[:, cols] - 0.7 * (clipped + 0.9 * fresh)
        copies += [
            pltpu.make_async_copy(momentum_out.at[i], new_momentum.at[:, cols], sems.at[0, i]),
            pltpu.make_async_copy(params_out.at[i], new_params.at[:, cols], sems.at[1, i]),
        ]
        copies[-2].start()
        copies[-1].start()
    for copy in copies:
        copy.wait()


def update(count, flips, averages, squares, params, momentum, earlier=()):
    rows, width = averages[0].shape
    out = jax.ShapeDtypeStruct(params.shape, WIDE)
    first = 3 + len(flips)
    return pl.pallas_call(
        functools.partial(update_kernel, count, flips, len(earlier)),
        out_shape=[out, out],
        in_specs=[VMEM] * first + [HBM] * len(earlier),
        out_specs=[HBM] * 2,
        scratch_shapes=[
            pltpu.VMEM((len(flips), rows, width), WIDE),
            pltpu.VMEM((len(flips), rows, width), WIDE),
            pltpu.SemaphoreType.DMA((2, len(flips))),
        ],
        input_output_aliases={first + i: i for i in range(len(earlier))},
        compiler_params=pltpu.CompilerParams(vmem_limit_bytes=LIMIT),
    )(squares, params, momentum, *averages, *earlier)


def per_device(pseudo_grad, params, momentum):
    groups = lax.axis_size("replica")
    devices = groups * lax.axis_size("fsdp")
    rows, columns = params.shape
    width = columns // groups
    count = rows * lax.axis_size("fsdp") * columns
    limit = pltpu.CompilerParams(vmem_limit_bytes=LIMIT)
    piece = jax.ShapeDtypeStruct((rows, width), pseudo_grad.dtype)
    pieces = pl.pallas_call(
        cut_kernel,
        out_shape=[piece] * groups,
        in_specs=[HBM],
        out_specs=[VMEM] * groups,
        scratch_shapes=[pltpu.SemaphoreType.DMA((groups,))],
        compiler_params=limit,
    )(pseudo_grad)
    pieces, params, momentum = lax.optimization_barrier((pieces, params, momentum))
    kept = jax.ShapeDtypeStruct(params.shape, WIDE)
    params, momentum = pl.pallas_call(
        fetch_kernel,
        out_shape=[kept, kept],
        in_specs=[HBM] * 2,
        out_specs=[VMEM] * 2,
        scratch_shapes=[pltpu.SemaphoreType.DMA((2,))],
        compiler_params=limit,
        cost_estimate=pl.CostEstimate(flops=0, bytes_accessed=8 * params.size, transcendentals=0),
    )(params, momentum)
    moved = {k: swapped(pieces[k], "replica", k) for k in range(2, groups)}
    near, params, momentum = lax.optimization_barrier((pieces[1], params, momentum))
    moved.update({0: pieces[0], 1: swapped(near, "replica", 1)})
    average, squares = pl.pallas_call(
        average_kernel,
        out_shape=[
            jax.ShapeDtypeStruct((rows, width), WIDE),
            jax.ShapeDtypeStruct((devices, 1, 128), WIDE),
        ],
        in_specs=[VMEM] * groups,
        out_specs=[VMEM] * 2,
        compiler_params=limit,
    )(*[moved[k] for k in range(groups)])
    averages = {0: average}
    for k in range(2, groups, 2):
        averages[k] = swapped(average, "replica", k)
    averages[1] = swapped(average, "replica", 1)
    middle = lax.axis_size("fsdp") // 2 + 1
    members = sorted(range(devices), key=lambda i: i != middle)
    squares = lax.all_to_all(
        squares,
        ("replica", "fsdp"),
        split_axis=0,
        concat_axis=0,
        axis_index_groups=[members],
        tiled=True,
    )
    squares, averages = lax.optimization_barrier((squares, averages))
    for k in range(2, groups, 2):
        averages[k + 1] = swapped(averages[k], "replica", 1)
    here = [k for k in range(groups) if k < 2 or k % 2 == 0]
    late = [k for k in range(groups) if k not in here]
    outs = update(count, here, [averages[k] for k in here], squares, params, momentum)
    if late:
        outs = update(
            count, late, [averages[k] for k in late], squares, params, momentum, outs
        )
    return outs


def solution(mesh):
    placed = (P("replica", "fsdp", None), P("fsdp", None), P("fsdp", None))
    return jax.shard_map(
        per_device,
        mesh=mesh,
        in_specs=placed,
        out_specs=(P("fsdp", None), P("fsdp", None)),
        check_vma=False,
    )
```

```python
import functools

import jax
import jax.numpy as jnp
from jax import lax
from jax.experimental import pallas as pl
from jax.experimental.pallas import tpu as pltpu
from jax.sharding import PartitionSpec as P

WIDE = jnp.float32
VMEM = pl.BlockSpec(memory_space=pltpu.VMEM)
HBM = pl.BlockSpec(memory_space=pltpu.HBM)
LIMIT = 16 * 1024 * 1024


def swapped(value, axis, flip):
    size = lax.axis_size(axis)
    return lax.ppermute(value, axis, [(i, i ^ flip) for i in range(size)])


def piece_of(k, width):
    return pl.ds(pl.multiple_of((lax.axis_index("replica") ^ k) * width, width), width)


def tree(parts):
    while len(parts) > 1:
        parts = [parts[i] + parts[i + 1] for i in range(0, len(parts), 2)]
    return parts[0]


def cut_kernel(flips, arrays, *refs):
    grad, sems = refs[0], refs[-1]
    outs = refs[1 + arrays : -1]
    moves = [(grad.at[0, :, piece_of(k, outs[0].shape[1])], out) for k, out in zip(flips, outs)]
    moves += list(zip(refs[1 : 1 + arrays], outs[len(flips) :]))
    copies = [
        pltpu.make_async_copy(source, out, sems.at[i])
        for i, (source, out) in enumerate(moves)
    ]
    for copy in copies:
        copy.start()
    for copy in copies:
        copy.wait()


def cut(grad, width, flips, *arrays):
    piece = jax.ShapeDtypeStruct((grad.shape[1], width), grad.dtype)
    out_shape = [piece] * len(flips) + [jax.ShapeDtypeStruct(x.shape, x.dtype) for x in arrays]
    held = [pltpu.with_memory_space_constraint(x, pltpu.HBM) for x in (grad, *arrays)]
    outs = pl.pallas_call(
        functools.partial(cut_kernel, flips, len(arrays)),
        out_shape=out_shape,
        in_specs=[HBM] * len(held),
        out_specs=[VMEM] * len(out_shape),
        scratch_shapes=[pltpu.SemaphoreType.DMA((len(out_shape),))],
        compiler_params=pltpu.CompilerParams(vmem_limit_bytes=LIMIT),
    )(*held)
    return dict(zip(flips, outs)), outs[len(flips) :]


def average_kernel(*refs):
    pieces, (average, squares) = refs[:-2], refs[-2:]
    total = tree([piece[...].astype(WIDE) for piece in pieces])
    mean = total / WIDE(len(pieces))
    average[...] = mean
    row = jnp.sum(mean * mean, axis=0, keepdims=True)
    lanes = functools.reduce(
        jnp.add, [row[:, i : i + 128] for i in range(0, row.shape[1], 128)]
    )
    squares[...] = jnp.broadcast_to(lanes[None], squares.shape)


def update_kernel(count, flips, passed, squares, params, momentum, *refs):
    averages, refs = refs[: len(flips)], refs[len(flips) + passed :]
    new_params, new_momentum, params_out, momentum_out, sems = refs
    square_sum = jnp.sum(squares[...], keepdims=True).reshape(1, 1)
    factor = 0.2 / jnp.sqrt(square_sum / WIDE(count) + 1e-06)
    width = averages[0].shape[1]
    copies = []
    for i, (k, average) in enumerate(zip(flips, averages)):
        cols = piece_of(k, width)
        clipped = factor * average[...]
        fresh = 0.9 * momentum[:, cols] + clipped
        momentum_out[i] = fresh
        params_out[i] = params[:, cols] - 0.7 * (clipped + 0.9 * fresh)
        copies += [
            pltpu.make_async_copy(momentum_out.at[i], new_momentum.at[:, cols], sems.at[0, i]),
            pltpu.make_async_copy(params_out.at[i], new_params.at[:, cols], sems.at[1, i]),
        ]
        copies[-2].start()
        copies[-1].start()
    for copy in copies:
        copy.wait()


def update(count, flips, averages, squares, params, momentum, earlier=()):
    rows, width = averages[0].shape
    out = jax.ShapeDtypeStruct(params.shape, WIDE)
    first = 3 + len(flips)
    return pl.pallas_call(
        functools.partial(update_kernel, count, flips, len(earlier)),
        out_shape=[out, out],
        in_specs=[VMEM] * first + [HBM] * len(earlier),
        out_specs=[HBM] * 2,
        scratch_shapes=[
            pltpu.VMEM((len(flips), rows, width), WIDE),
            pltpu.VMEM((len(flips), rows, width), WIDE),
            pltpu.SemaphoreType.DMA((2, len(flips))),
        ],
        input_output_aliases={first + i: i for i in range(len(earlier))},
        compiler_params=pltpu.CompilerParams(vmem_limit_bytes=LIMIT),
    )(squares, params, momentum, *averages, *earlier)


def per_device(pseudo_grad, params, momentum):
    groups = lax.axis_size("replica")
    devices = groups * lax.axis_size("fsdp")
    rows, columns = params.shape
    width = columns // groups
    count = rows * lax.axis_size("fsdp") * columns
    limit = pltpu.CompilerParams(vmem_limit_bytes=LIMIT)
    pieces, _ = cut(pseudo_grad, width, range(2, groups))
    pieces, pseudo_grad, params, momentum = lax.optimization_barrier(
        (pieces, pseudo_grad, params, momentum)
    )
    moved = {k: swapped(pieces[k], "replica", k) for k in range(2, groups)}
    near, (params, momentum) = cut(pseudo_grad, width, range(2), params, momentum)
    moved.update({0: near[0], 1: swapped(near[1], "replica", 1)})
    average, squares = pl.pallas_call(
        average_kernel,
        out_shape=[
            jax.ShapeDtypeStruct((rows, width), WIDE),
            jax.ShapeDtypeStruct((devices, 1, 128), WIDE),
        ],
        in_specs=[VMEM] * groups,
        out_specs=[VMEM] * 2,
        compiler_params=limit,
    )(*[moved[k] for k in range(groups)])
    averages = {0: average}
    for k in range(2, groups, 2):
        averages[k] = swapped(average, "replica", k)
    averages[1] = swapped(average, "replica", 1)
    squares = lax.all_to_all(
        squares, ("replica", "fsdp"), split_axis=0, concat_axis=0, tiled=True
    )
    squares, averages = lax.optimization_barrier((squares, averages))
    for k in range(2, groups, 2):
        averages[k + 1] = swapped(averages[k], "replica", 1)
    here = [k for k in range(groups) if k < 2 or k % 2 == 0]
    late = [k for k in range(groups) if k not in here]
    outs = update(count, here, [averages[k] for k in here], squares, params, momentum)
    if late:
        outs = update(
            count, late, [averages[k] for k in late], squares, params, momentum, outs
        )
    return outs


def solution(mesh):
    placed = (P("replica", "fsdp", None), P("fsdp", None), P("fsdp", None))
    return jax.shard_map(
        per_device,
        mesh=mesh,
        in_specs=placed,
        out_specs=(P("fsdp", None), P("fsdp", None)),
        check_vma=False,
    )
```

```python
import functools

import jax
import jax.numpy as jnp
from jax import lax
from jax.experimental import pallas as pl
from jax.experimental.pallas import tpu as pltpu
from jax.sharding import PartitionSpec as P

WIDE = jnp.float32
VMEM = pl.BlockSpec(memory_space=pltpu.VMEM)
HBM = pl.BlockSpec(memory_space=pltpu.HBM)
LIMIT = 16 * 1024 * 1024


def swapped(value, axis, flip):
    size = lax.axis_size(axis)
    return lax.ppermute(value, axis, [(i, i ^ flip) for i in range(size)])


def piece_of(k, width):
    return pl.ds(pl.multiple_of((lax.axis_index("replica") ^ k) * width, width), width)


SIDE = 128
TOP = 2.0**7.5
KNEE = 2.0**-4


def encode(value):
    size = jnp.abs(value)
    scale = jnp.maximum(jnp.max(size, axis=1, keepdims=True), 1e-30)
    scale = scale.astype(jnp.bfloat16).astype(WIDE)
    unit = size * (TOP / scale)
    power = unit
    for _ in range(4):
        power = power * power
    code = jnp.where(unit < KNEE, unit * KNEE**15, power)
    code = jnp.where(value < 0, -code, code).astype(jnp.bfloat16)
    side = jnp.broadcast_to(scale, (value.shape[0], SIDE)).astype(jnp.bfloat16)
    return jnp.concatenate([code, side], axis=1)


def decode(code):
    width = code.shape[1] - SIDE
    scale = code[:, width : width + 1].astype(WIDE)
    power = code[:, :width].astype(WIDE)
    size = jnp.abs(power)
    root = jnp.exp(jnp.log(jnp.maximum(size, KNEE**16)) * (1 / 16))
    unit = jnp.where(size < KNEE**16, size * KNEE**-15, root) * (scale * (1 / TOP))
    return jnp.where(power < 0, -unit, unit)


def tree(parts):
    while len(parts) > 1:
        parts = [parts[i] + parts[i + 1] for i in range(0, len(parts), 2)]
    return parts[0]


def copy_all(moves, sems):
    copies = [
        pltpu.make_async_copy(source, out, sems.at[i])
        for i, (source, out) in enumerate(moves)
    ]
    for copy in copies:
        copy.start()
    for copy in copies:
        copy.wait()


def cut_kernel(flips, grad, *refs):
    outs, sems = refs[:-1], refs[-1]
    width = outs[0].shape[2]
    copy_all(
        [
            (grad.at[0, :, piece_of(k, width)], out.at[i])
            for group, out in zip(flips, outs)
            for i, k in enumerate(group)
        ],
        sems,
    )


def read_kernel(*refs):
    count = len(refs) // 2
    copy_all(list(zip(refs[:count], refs[count:-1])), refs[-1])


def call(kernel, out_shape, *args, held=False, copies=0):
    if held:
        args = [pltpu.with_memory_space_constraint(x, pltpu.HBM) for x in args]
    return pl.pallas_call(
        kernel,
        out_shape=out_shape,
        in_specs=[HBM if held else VMEM] * len(args),
        out_specs=[VMEM] * len(out_shape),
        scratch_shapes=[pltpu.SemaphoreType.DMA((copies,))] if copies else (),
        compiler_params=pltpu.CompilerParams(vmem_limit_bytes=LIMIT),
    )(*args)


def cut(grad, width, *flips):
    out_shape = [
        jax.ShapeDtypeStruct((len(group), grad.shape[1], width), grad.dtype)
        for group in flips
    ]
    kernel = functools.partial(cut_kernel, flips)
    return call(kernel, out_shape, grad, held=True, copies=sum(map(len, flips)))


def read(*arrays):
    out_shape = [jax.ShapeDtypeStruct(x.shape, x.dtype) for x in arrays]
    return call(read_kernel, out_shape, *arrays, held=True, copies=len(arrays))


def squares_of(mean, squares):
    row = jnp.sum(mean * mean, axis=0, keepdims=True)
    lanes = functools.reduce(
        jnp.add, [row[:, i : i + 128] for i in range(0, row.shape[1], 128)]
    )
    squares[...] = jnp.broadcast_to(lanes[None], squares.shape)


def average_kernel(*refs):
    pieces, (average, squares) = refs[:-2], refs[-2:]
    total = tree([piece[...].astype(WIDE) for piece in pieces])
    mean = total / WIDE(len(pieces))
    average[...] = mean
    squares_of(mean, squares)


def pair_kernel(own, mate, first, second, sums):
    for i, code in enumerate((first, second)):
        code[...] = encode(own[i].astype(WIDE) + mate[i].astype(WIDE))
        sums[i] = decode(code[...])


def join_kernel(groups, sums, code, average, squares):
    mean = (sums[0] + decode(code[...])) / WIDE(groups)
    average[...] = mean
    squares_of(mean, squares)


def write_out(count, flips, means, squares, params, momentum, refs):
    new_params, new_momentum, params_out, momentum_out, sems = refs
    square_sum = jnp.sum(squares[...], keepdims=True).reshape(1, 1)
    factor = 0.2 / jnp.sqrt(square_sum / WIDE(count) + 1e-06)
    width = params_out.shape[2]
    copies = []
    for i, (k, mean) in enumerate(zip(flips, means)):
        cols = piece_of(k, width)
        clipped = factor * mean()
        fresh = 0.9 * momentum[:, cols] + clipped
        momentum_out[i] = fresh
        params_out[i] = params[:, cols] - 0.7 * (clipped + 0.9 * fresh)
        copies += [
            pltpu.make_async_copy(momentum_out.at[i], new_momentum.at[:, cols], sems.at[0, i]),
            pltpu.make_async_copy(params_out.at[i], new_params.at[:, cols], sems.at[1, i]),
        ]
        copies[-2].start()
        copies[-1].start()
    for copy in copies:
        copy.wait()


def update_kernel(count, flips, passed, squares, params, momentum, *refs):
    means = [functools.partial(ref.__getitem__, ...) for ref in refs[: len(flips)]]
    write_out(count, flips, means, squares, params, momentum, refs[len(flips) + passed :])


def final_kernel(count, groups, squares, params, momentum, average, own, mate, one, two, three, *refs):
    def joined(sums, i, code):
        return lambda: (sums[i] + decode(code[...])) / WIDE(groups)

    means = [
        functools.partial(average.__getitem__, ...),
        joined(mate, 0, one),
        joined(own, 1, two),
        joined(mate, 1, three),
    ]
    write_out(count, range(groups), means, squares, params, momentum, refs)


def update(kernel, flips, width, args, earlier=()):
    shape = args[1].shape
    out = jax.ShapeDtypeStruct(shape, WIDE)
    return pl.pallas_call(
        kernel,
        out_shape=[out, out],
        in_specs=[VMEM] * len(args) + [HBM] * len(earlier),
        out_specs=[HBM] * 2,
        scratch_shapes=[
            pltpu.VMEM((len(flips), shape[0], width), WIDE),
            pltpu.VMEM((len(flips), shape[0], width), WIDE),
            pltpu.SemaphoreType.DMA((2, len(flips))),
        ],
        input_output_aliases={len(args) + i: i for i in range(len(earlier))},
        compiler_params=pltpu.CompilerParams(vmem_limit_bytes=LIMIT),
    )(*args, *earlier)


def all_squares(squares):
    return lax.all_to_all(
        squares, ("replica", "fsdp"), split_axis=0, concat_axis=0, tiled=True
    )


def two_chips(pseudo_grad, params, momentum, width, count, square_rows):
    groups = lax.axis_size("replica")
    rows = params.shape[0]
    code = jax.ShapeDtypeStruct((rows, width + SIDE), jnp.bfloat16)
    sums = jax.ShapeDtypeStruct((2, rows, width), WIDE)
    own, others = cut(pseudo_grad, width, (0, 2), (1, 3))
    mate = swapped(others, "replica", 1)
    code_own, code_far, own_sums = call(pair_kernel, [code, code, sums], own, mate)
    urgent = swapped(code_far, "replica", 2)
    mate_sums = swapped(own_sums, "replica", 1)
    code_own, code_far, params, momentum = lax.optimization_barrier(
        (code_own, code_far, params, momentum)
    )
    params, momentum = read(params, momentum)
    code_own, code_far, params, momentum = lax.optimization_barrier(
        (code_own, code_far, params, momentum)
    )
    one = swapped(code_far, "replica", 3)
    two = swapped(code_own, "replica", 2)
    three = swapped(code_own, "replica", 3)
    average, squares = call(
        functools.partial(join_kernel, groups),
        [jax.ShapeDtypeStruct((rows, width), WIDE), square_rows],
        own_sums, urgent,
    )
    squares = all_squares(squares)
    squares, one, two, three, mate_sums = lax.optimization_barrier(
        (squares, one, two, three, mate_sums)
    )
    return update(
        functools.partial(final_kernel, count, groups), range(groups), width,
        (squares, params, momentum, average, own_sums, mate_sums, one, two, three),
    )


def per_device(pseudo_grad, params, momentum):
    groups = lax.axis_size("replica")
    devices = groups * lax.axis_size("fsdp")
    rows, columns = params.shape
    width = columns // groups
    count = rows * lax.axis_size("fsdp") * columns
    square_rows = jax.ShapeDtypeStruct((devices, 1, 128), WIDE)
    if groups == 4:
        return two_chips(pseudo_grad, params, momentum, width, count, square_rows)
    (pieces,) = cut(pseudo_grad, width, range(groups))
    params, momentum = read(params, momentum)
    moved = [swapped(pieces[k], "replica", k) if k else pieces[k] for k in range(groups)]
    average, squares = call(
        average_kernel, [jax.ShapeDtypeStruct((rows, width), WIDE), square_rows], *moved
    )
    averages = {0: average, 1: swapped(average, "replica", 1)}
    for k in range(2, groups, 2):
        averages[k] = swapped(average, "replica", k)
    squares = all_squares(squares)
    squares, averages = lax.optimization_barrier((squares, averages))
    for k in range(2, groups, 2):
        averages[k + 1] = swapped(averages[k], "replica", 1)
    here = [k for k in range(groups) if k < 2 or k % 2 == 0]
    late = [k for k in range(groups) if k not in here]
    outs = ()
    for flips in (here, late):
        if flips:
            outs = update(
                functools.partial(update_kernel, count, flips, len(outs)), flips, width,
                (squares, params, momentum, *[averages[k] for k in flips]), outs,
            )
    return outs


def solution(mesh):
    placed = (P("replica", "fsdp", None), P("fsdp", None), P("fsdp", None))
    return jax.shard_map(
        per_device,
        mesh=mesh,
        in_specs=placed,
        out_specs=(P("fsdp", None), P("fsdp", None)),
        check_vma=False,
    )
```

```python
import functools

import jax
import jax.numpy as jnp
from jax import lax
from jax.experimental import pallas as pl
from jax.experimental.pallas import tpu as pltpu
from jax.sharding import PartitionSpec as P

WIDE = jnp.float32
VMEM = pl.BlockSpec(memory_space=pltpu.VMEM)
HBM = pl.BlockSpec(memory_space=pltpu.HBM)
LIMIT = 16 * 1024 * 1024


def swapped(value, axis, flip):
    size = lax.axis_size(axis)
    return lax.ppermute(value, axis, [(i, i ^ flip) for i in range(size)])


def piece_of(k, width):
    return pl.ds(pl.multiple_of((lax.axis_index("replica") ^ k) * width, width), width)


def tree(parts):
    while len(parts) > 1:
        parts = [parts[i] + parts[i + 1] for i in range(0, len(parts), 2)]
    return parts[0]


def cut_kernel(flips, arrays, *refs):
    grad, sems = refs[0], refs[-1]
    outs = refs[1 + arrays : -1]
    moves = [(grad.at[0, :, piece_of(k, outs[0].shape[1])], out) for k, out in zip(flips, outs)]
    moves += list(zip(refs[1 : 1 + arrays], outs[len(flips) :]))
    copies = [
        pltpu.make_async_copy(source, out, sems.at[i])
        for i, (source, out) in enumerate(moves)
    ]
    for copy in copies:
        copy.start()
    for copy in copies:
        copy.wait()


def cut(grad, width, flips, *arrays):
    piece = jax.ShapeDtypeStruct((grad.shape[1], width), grad.dtype)
    out_shape = [piece] * len(flips) + [jax.ShapeDtypeStruct(x.shape, x.dtype) for x in arrays]
    held = [pltpu.with_memory_space_constraint(x, pltpu.HBM) for x in (grad, *arrays)]
    outs = pl.pallas_call(
        functools.partial(cut_kernel, flips, len(arrays)),
        out_shape=out_shape,
        in_specs=[HBM] * len(held),
        out_specs=[VMEM] * len(out_shape),
        scratch_shapes=[pltpu.SemaphoreType.DMA((len(out_shape),))],
        compiler_params=pltpu.CompilerParams(vmem_limit_bytes=LIMIT),
    )(*held)
    return dict(zip(flips, outs)), outs[len(flips) :]


def average_kernel(*refs):
    pieces, (average, squares) = refs[:-2], refs[-2:]
    total = tree([piece[...].astype(WIDE) for piece in pieces])
    mean = total / WIDE(len(pieces))
    average[...] = mean
    row = jnp.sum(mean * mean, axis=0, keepdims=True)
    lanes = functools.reduce(
        jnp.add, [row[:, i : i + 128] for i in range(0, row.shape[1], 128)]
    )
    squares[...] = jnp.broadcast_to(lanes[None], squares.shape)


def update_kernel(count, flips, squares, params, momentum, *refs):
    averages, refs = refs[: len(flips)], refs[len(flips) :]
    new_params, new_momentum, params_out, momentum_out, sems = refs
    square_sum = jnp.sum(squares[...], keepdims=True).reshape(1, 1)
    factor = 0.2 / jnp.sqrt(square_sum / WIDE(count) + 1e-06)
    width = averages[0].shape[1]
    copies = []
    for i, (k, average) in enumerate(zip(flips, averages)):
        cols = piece_of(k, width)
        clipped = factor * average[...]
        fresh = 0.9 * momentum[:, cols] + clipped
        momentum_out[i] = fresh
        params_out[i] = params[:, cols] - 0.7 * (clipped + 0.9 * fresh)
        copies += [
            pltpu.make_async_copy(momentum_out.at[i], new_momentum.at[:, cols], sems.at[0, i]),
            pltpu.make_async_copy(params_out.at[i], new_params.at[:, cols], sems.at[1, i]),
        ]
        copies[-2].start()
        copies[-1].start()
    for copy in copies:
        copy.wait()


def update(count, flips, averages, squares, params, momentum):
    rows, width = averages[0].shape
    out = jax.ShapeDtypeStruct(params.shape, WIDE)
    return pl.pallas_call(
        functools.partial(update_kernel, count, flips),
        out_shape=[out, out],
        in_specs=[VMEM] * (3 + len(flips)),
        out_specs=[HBM] * 2,
        scratch_shapes=[
            pltpu.VMEM((len(flips), rows, width), WIDE),
            pltpu.VMEM((len(flips), rows, width), WIDE),
            pltpu.SemaphoreType.DMA((2, len(flips))),
        ],
        compiler_params=pltpu.CompilerParams(vmem_limit_bytes=LIMIT),
    )(squares, params, momentum, *averages)


def per_device(pseudo_grad, params, momentum):
    groups = lax.axis_size("replica")
    devices = groups * lax.axis_size("fsdp")
    rows, columns = params.shape
    width = columns // groups
    count = rows * lax.axis_size("fsdp") * columns
    limit = pltpu.CompilerParams(vmem_limit_bytes=LIMIT)
    pieces, _ = cut(pseudo_grad, width, range(2, groups))
    pieces, pseudo_grad, params, momentum = lax.optimization_barrier(
        (pieces, pseudo_grad, params, momentum)
    )
    moved = {k: swapped(pieces[k], "replica", k) for k in range(2, groups)}
    near, (params, momentum) = cut(pseudo_grad, width, range(2), params, momentum)
    moved.update({0: near[0], 1: swapped(near[1], "replica", 1)})
    average, squares = pl.pallas_call(
        average_kernel,
        out_shape=[
            jax.ShapeDtypeStruct((rows, width), WIDE),
            jax.ShapeDtypeStruct((devices, 1, 128), WIDE),
        ],
        in_specs=[VMEM] * groups,
        out_specs=[VMEM] * 2,
        compiler_params=limit,
    )(*[moved[k] for k in range(groups)])
    averages = {0: average}
    for k in range(2, groups, 2):
        averages[k] = swapped(average, "replica", k)
    averages[1] = swapped(average, "replica", 1)
    squares = lax.all_to_all(
        squares, ("replica", "fsdp"), split_axis=0, concat_axis=0, tiled=True
    )
    for k in range(2, groups, 2):
        averages[k + 1] = swapped(averages[k], "replica", 1)
    return update(
        count, range(groups), [averages[k] for k in range(groups)], squares, params, momentum
    )


def solution(mesh):
    placed = (P("replica", "fsdp", None), P("fsdp", None), P("fsdp", None))
    return jax.shard_map(
        per_device,
        mesh=mesh,
        in_specs=placed,
        out_specs=(P("fsdp", None), P("fsdp", None)),
        check_vma=False,
    )
```

```python
import functools

import jax
import jax.numpy as jnp
from jax import lax
from jax.experimental import pallas as pl
from jax.experimental.pallas import tpu as pltpu
from jax.sharding import PartitionSpec as P

WIDE = jnp.float32
VMEM = pl.BlockSpec(memory_space=pltpu.VMEM)
HBM = pl.BlockSpec(memory_space=pltpu.HBM)
LIMIT = 16 * 1024 * 1024


def swapped(value, axis, flip):
    size = lax.axis_size(axis)
    return lax.ppermute(value, axis, [(i, i ^ flip) for i in range(size)])


def piece_of(k, width):
    return pl.ds(pl.multiple_of((lax.axis_index("replica") ^ k) * width, width), width)


SIDE = 128
TOP = 2.0**7.5
KNEE = 2.0**-4


def encode(value):
    size = jnp.abs(value)
    scale = jnp.maximum(jnp.max(size, axis=1, keepdims=True), 1e-30)
    scale = scale.astype(jnp.bfloat16).astype(WIDE)
    unit = size * (TOP / scale)
    power = unit
    for _ in range(4):
        power = power * power
    code = jnp.where(unit < KNEE, unit * KNEE**15, power)
    code = jnp.where(value < 0, -code, code).astype(jnp.bfloat16)
    side = jnp.broadcast_to(scale, (value.shape[0], SIDE)).astype(jnp.bfloat16)
    return jnp.concatenate([code, side], axis=1)


def decode(code):
    width = code.shape[1] - SIDE
    scale = code[:, width : width + 1].astype(WIDE)
    power = code[:, :width].astype(WIDE)
    size = jnp.abs(power)
    root = jnp.maximum(size, KNEE**16)
    for _ in range(4):
        root = lax.rsqrt(root)
    unit = jnp.where(size < KNEE**16, size * KNEE**-15, root) * (scale * (1 / TOP))
    return jnp.where(power < 0, -unit, unit)


def tree(parts):
    while len(parts) > 1:
        parts = [parts[i] + parts[i + 1] for i in range(0, len(parts), 2)]
    return parts[0]


def copy_all(moves, sems):
    copies = [
        pltpu.make_async_copy(source, out, sems.at[i])
        for i, (source, out) in enumerate(moves)
    ]
    for copy in copies:
        copy.start()
    for copy in copies:
        copy.wait()


def cut_kernel(flips, grad, *refs):
    outs, sems = refs[:-1], refs[-1]
    width = outs[0].shape[2]
    copy_all(
        [
            (grad.at[0, :, piece_of(k, width)], out.at[i])
            for group, out in zip(flips, outs)
            for i, k in enumerate(group)
        ],
        sems,
    )


def read_kernel(*refs):
    count = len(refs) // 2
    copy_all(list(zip(refs[:count], refs[count:-1])), refs[-1])


def call(kernel, out_shape, *args, held=False, copies=0):
    if held:
        args = [pltpu.with_memory_space_constraint(x, pltpu.HBM) for x in args]
    return pl.pallas_call(
        kernel,
        out_shape=out_shape,
        in_specs=[HBM if held else VMEM] * len(args),
        out_specs=[VMEM] * len(out_shape),
        scratch_shapes=[pltpu.SemaphoreType.DMA((copies,))] if copies else (),
        compiler_params=pltpu.CompilerParams(vmem_limit_bytes=LIMIT),
    )(*args)


def cut(grad, width, *flips):
    out_shape = [
        jax.ShapeDtypeStruct((len(group), grad.shape[1], width), grad.dtype)
        for group in flips
    ]
    kernel = functools.partial(cut_kernel, flips)
    return call(kernel, out_shape, grad, held=True, copies=sum(map(len, flips)))


def read(*arrays):
    out_shape = [jax.ShapeDtypeStruct(x.shape, x.dtype) for x in arrays]
    return call(read_kernel, out_shape, *arrays, held=True, copies=len(arrays))


def squares_of(mean, squares):
    row = jnp.sum(mean * mean, axis=0, keepdims=True)
    lanes = functools.reduce(
        jnp.add, [row[:, i : i + 128] for i in range(0, row.shape[1], 128)]
    )
    squares[...] = jnp.broadcast_to(lanes[None], squares.shape)


def average_kernel(*refs):
    pieces, (average, squares) = refs[:-2], refs[-2:]
    total = tree([piece[...].astype(WIDE) for piece in pieces])
    mean = total / WIDE(len(pieces))
    average[...] = mean
    squares_of(mean, squares)


def pair_sum(own, mate, i):
    return own[i].astype(WIDE) + mate[i].astype(WIDE)


def urgent_kernel(own, mate, code):
    code[...] = encode(pair_sum(own, mate, 1))


def pair_kernel(own, mate, urgent, code, sum_own, sum_far):
    code[...] = encode(pair_sum(own, mate, 0))
    sum_own[...] = decode(code[...])
    sum_far[...] = decode(urgent[...])


def first_kernel(groups, sums, code, average, squares):
    mean = (sums[...] + decode(code[...])) / WIDE(groups)
    average[...] = mean
    squares_of(mean, squares)


def join_kernel(groups, *refs):
    for sums, code, average in zip(refs[:3], refs[3:6], refs[6:]):
        average[...] = (sums[...] + decode(code[...])) / WIDE(groups)


def write_out(count, flips, means, squares, params, momentum, refs):
    new_params, new_momentum, params_out, momentum_out, sems = refs
    square_sum = jnp.sum(squares[...], keepdims=True).reshape(1, 1)
    factor = 0.2 / jnp.sqrt(square_sum / WIDE(count) + 1e-06)
    width = params_out.shape[2]
    copies = []
    for i, (k, mean) in enumerate(zip(flips, means)):
        cols = piece_of(k, width)
        clipped = factor * mean()
        fresh = 0.9 * momentum[:, cols] + clipped
        momentum_out[i] = fresh
        params_out[i] = params[:, cols] - 0.7 * (clipped + 0.9 * fresh)
        copies += [
            pltpu.make_async_copy(momentum_out.at[i], new_momentum.at[:, cols], sems.at[0, i]),
            pltpu.make_async_copy(params_out.at[i], new_params.at[:, cols], sems.at[1, i]),
        ]
        copies[-2].start()
        copies[-1].start()
    for copy in copies:
        copy.wait()


def update_kernel(count, flips, passed, squares, params, momentum, *refs):
    means = [functools.partial(ref.__getitem__, ...) for ref in refs[: len(flips)]]
    write_out(count, flips, means, squares, params, momentum, refs[len(flips) + passed :])


def update(kernel, flips, width, args, earlier=()):
    shape = args[1].shape
    out = jax.ShapeDtypeStruct(shape, WIDE)
    return pl.pallas_call(
        kernel,
        out_shape=[out, out],
        in_specs=[VMEM] * len(args) + [HBM] * len(earlier),
        out_specs=[HBM] * 2,
        scratch_shapes=[
            pltpu.VMEM((len(flips), shape[0], width), WIDE),
            pltpu.VMEM((len(flips), shape[0], width), WIDE),
            pltpu.SemaphoreType.DMA((2, len(flips))),
        ],
        input_output_aliases={len(args) + i: i for i in range(len(earlier))},
        compiler_params=pltpu.CompilerParams(vmem_limit_bytes=LIMIT),
    )(*args, *earlier)


def all_squares(squares):
    return lax.all_to_all(
        squares, ("replica", "fsdp"), split_axis=0, concat_axis=0, tiled=True
    )


def two_chips(pseudo_grad, params, momentum, width, count, square_rows):
    groups = lax.axis_size("replica")
    rows = params.shape[0]
    code = jax.ShapeDtypeStruct((rows, width + SIDE), jnp.bfloat16)
    piece = jax.ShapeDtypeStruct((rows, width), WIDE)
    own, others = cut(pseudo_grad, width, (0, 2), (1, 3))
    mate = swapped(others, "replica", 1)
    (code_far,) = call(urgent_kernel, [code], own, mate)
    urgent = swapped(code_far, "replica", 2)
    own, mate, code_far, params, momentum = lax.optimization_barrier(
        (own, mate, code_far, params, momentum)
    )
    params, momentum = read(params, momentum)
    own, mate, code_far, params, momentum = lax.optimization_barrier(
        (own, mate, code_far, params, momentum)
    )
    code_own, sum_own, sum_far = call(
        pair_kernel, [code, piece, piece], own, mate, code_far
    )
    mate_own, mate_far = (swapped(x, "replica", 1) for x in (sum_own, sum_far))
    one = swapped(code_far, "replica", 3)
    two = swapped(code_own, "replica", 2)
    three = swapped(code_own, "replica", 3)
    average, squares = call(
        functools.partial(first_kernel, groups), [piece, square_rows], sum_own, urgent
    )
    squares = all_squares(squares)
    joined = call(
        functools.partial(join_kernel, groups), [piece] * 3,
        mate_own, sum_far, mate_far, one, two, three,
    )
    flips = range(groups)
    return update(
        functools.partial(update_kernel, count, flips, 0), flips, width,
        (squares, params, momentum, average, *joined),
    )


def per_device(pseudo_grad, params, momentum):
    groups = lax.axis_size("replica")
    devices = groups * lax.axis_size("fsdp")
    rows, columns = params.shape
    width = columns // groups
    count = rows * lax.axis_size("fsdp") * columns
    square_rows = jax.ShapeDtypeStruct((devices, 1, 128), WIDE)
    if groups == 4:
        return two_chips(pseudo_grad, params, momentum, width, count, square_rows)
    (pieces,) = cut(pseudo_grad, width, range(groups))
    params, momentum = read(params, momentum)
    moved = [swapped(pieces[k], "replica", k) if k else pieces[k] for k in range(groups)]
    average, squares = call(
        average_kernel, [jax.ShapeDtypeStruct((rows, width), WIDE), square_rows], *moved
    )
    averages = {0: average, 1: swapped(average, "replica", 1)}
    for k in range(2, groups, 2):
        averages[k] = swapped(average, "replica", k)
    squares = all_squares(squares)
    squares, averages = lax.optimization_barrier((squares, averages))
    for k in range(2, groups, 2):
        averages[k + 1] = swapped(averages[k], "replica", 1)
    here = [k for k in range(groups) if k < 2 or k % 2 == 0]
    late = [k for k in range(groups) if k not in here]
    outs = ()
    for flips in (here, late):
        if flips:
            outs = update(
                functools.partial(update_kernel, count, flips, len(outs)), flips, width,
                (squares, params, momentum, *[averages[k] for k in flips]), outs,
            )
    return outs


def solution(mesh):
    placed = (P("replica", "fsdp", None), P("fsdp", None), P("fsdp", None))
    return jax.shard_map(
        per_device,
        mesh=mesh,
        in_specs=placed,
        out_specs=(P("fsdp", None), P("fsdp", None)),
        check_vma=False,
    )
```

```python
import functools

import jax
import jax.numpy as jnp
from jax import lax
from jax.experimental import pallas as pl
from jax.experimental.pallas import tpu as pltpu
from jax.sharding import PartitionSpec as P

WIDE = jnp.float32
VMEM = pl.BlockSpec(memory_space=pltpu.VMEM)
HBM = pl.BlockSpec(memory_space=pltpu.HBM)
LIMIT = 16 * 1024 * 1024


def swapped(value, axis, flip):
    size = lax.axis_size(axis)
    return lax.ppermute(value, axis, [(i, i ^ flip) for i in range(size)])


def piece_of(k, width):
    return pl.ds(pl.multiple_of((lax.axis_index("replica") ^ k) * width, width), width)


def tree(parts):
    while len(parts) > 1:
        parts = [parts[i] + parts[i + 1] for i in range(0, len(parts), 2)]
    return parts[0]


def cut_kernel(flips, arrays, *refs):
    grad, sems = refs[0], refs[-1]
    outs = refs[1 + arrays : -1]
    moves = [(grad.at[0, :, piece_of(k, outs[0].shape[1])], out) for k, out in zip(flips, outs)]
    moves += list(zip(refs[1 : 1 + arrays], outs[len(flips) :]))
    copies = [
        pltpu.make_async_copy(source, out, sems.at[i])
        for i, (source, out) in enumerate(moves)
    ]
    for copy in copies:
        copy.start()
    for copy in copies:
        copy.wait()


def cut(grad, width, flips, *arrays):
    piece = jax.ShapeDtypeStruct((grad.shape[1], width), grad.dtype)
    out_shape = [piece] * len(flips) + [jax.ShapeDtypeStruct(x.shape, x.dtype) for x in arrays]
    held = [pltpu.with_memory_space_constraint(x, pltpu.HBM) for x in (grad, *arrays)]
    outs = pl.pallas_call(
        functools.partial(cut_kernel, flips, len(arrays)),
        out_shape=out_shape,
        in_specs=[HBM] * len(held),
        out_specs=[VMEM] * len(out_shape),
        scratch_shapes=[pltpu.SemaphoreType.DMA((len(out_shape),))],
        compiler_params=pltpu.CompilerParams(vmem_limit_bytes=LIMIT),
    )(*held)
    return dict(zip(flips, outs)), outs[len(flips) :]


def average_kernel(*refs):
    pieces, (average, squares) = refs[:-2], refs[-2:]
    mean = tree([piece[...].astype(WIDE) for piece in pieces]) / WIDE(len(pieces))
    average[...] = mean
    row = jnp.sum(mean * mean, axis=0, keepdims=True)
    lanes = functools.reduce(
        jnp.add, [row[:, i : i + 128] for i in range(0, row.shape[1], 128)]
    )
    squares[...] = jnp.broadcast_to(lanes[None], squares.shape)


def join_kernel(*refs):
    pieces = [piece[...].astype(WIDE) for piece in refs[:-1]]
    refs[-1][...] = tree(pieces) / WIDE(len(pieces))


def update_kernel(count, flips, passed, squares, params, momentum, *refs):
    averages, refs = refs[: len(flips)], refs[len(flips) + passed :]
    new_params, new_momentum, params_out, momentum_out, sems = refs
    square_sum = jnp.sum(squares[...], keepdims=True).reshape(1, 1)
    factor = 0.2 / jnp.sqrt(square_sum / WIDE(count) + 1e-06)
    width = averages[0].shape[1]
    copies = []
    for i, (k, average) in enumerate(zip(flips, averages)):
        cols = piece_of(k, width)
        clipped = factor * average[...]
        fresh = 0.9 * momentum[:, cols] + clipped
        momentum_out[i] = fresh
        params_out[i] = params[:, cols] - 0.7 * (clipped + 0.9 * fresh)
        copies += [
            pltpu.make_async_copy(momentum_out.at[i], new_momentum.at[:, cols], sems.at[0, i]),
            pltpu.make_async_copy(params_out.at[i], new_params.at[:, cols], sems.at[1, i]),
        ]
        copies[-2].start()
        copies[-1].start()
    for copy in copies:
        copy.wait()


def update(count, flips, averages, squares, params, momentum, earlier=()):
    rows, width = averages[0].shape
    out = jax.ShapeDtypeStruct(params.shape, WIDE)
    first = 3 + len(flips)
    return pl.pallas_call(
        functools.partial(update_kernel, count, flips, len(earlier)),
        out_shape=[out, out],
        in_specs=[VMEM] * first + [HBM] * len(earlier),
        out_specs=[HBM] * 2,
        scratch_shapes=[
            pltpu.VMEM((len(flips), rows, width), WIDE),
            pltpu.VMEM((len(flips), rows, width), WIDE),
            pltpu.SemaphoreType.DMA((2, len(flips))),
        ],
        input_output_aliases={first + i: i for i in range(len(earlier))},
        compiler_params=pltpu.CompilerParams(vmem_limit_bytes=LIMIT),
    )(squares, params, momentum, *averages, *earlier)


def per_device(pseudo_grad, params, momentum):
    groups = lax.axis_size("replica")
    devices = groups * lax.axis_size("fsdp")
    rows, columns = params.shape
    width = columns // groups
    count = rows * lax.axis_size("fsdp") * columns
    limit = pltpu.CompilerParams(vmem_limit_bytes=LIMIT)
    pieces, _ = cut(pseudo_grad, width, range(2, groups))
    pieces, pseudo_grad, params, momentum = lax.optimization_barrier(
        (pieces, pseudo_grad, params, momentum)
    )
    moved = {k: swapped(pieces[k], "replica", k) for k in range(2, groups)}
    near, (params,) = cut(pseudo_grad, width, range(2), params)
    moved.update({0: near[0], 1: swapped(near[1], "replica", 1)})
    again = {}
    if groups == 4:
        near, params, momentum = lax.optimization_barrier((near, params, momentum))
        _, (momentum,) = cut(pseudo_grad, width, (), momentum)
        near, params, momentum = lax.optimization_barrier((near, params, momentum))
        again = {k: swapped(near[k ^ 2], "replica", k) for k in (2, 3)}
        again[1] = swapped(pieces[3], "replica", 1)
    else:
        _, (momentum,) = cut(pseudo_grad, width, (), momentum)
    average, squares = pl.pallas_call(
        average_kernel,
        out_shape=[
            jax.ShapeDtypeStruct((rows, width), WIDE),
            jax.ShapeDtypeStruct((devices, 1, 128), WIDE),
        ],
        in_specs=[VMEM] * groups,
        out_specs=[VMEM] * 2,
        compiler_params=limit,
    )(*[moved[k] for k in range(groups)])
    averages = {0: average}
    if groups != 4:
        averages.update({k: swapped(average, "replica", k) for k in range(2, groups, 2)})
    squares = lax.all_to_all(
        squares, ("replica", "fsdp"), split_axis=0, concat_axis=0, tiled=True
    )
    squares, averages, again = lax.optimization_barrier((squares, averages, again))
    if groups == 4:
        averages[2] = pl.pallas_call(
            join_kernel,
            out_shape=jax.ShapeDtypeStruct((rows, width), WIDE),
            in_specs=[VMEM] * groups,
            out_specs=VMEM,
            compiler_params=limit,
        )(again[2], again[3], pieces[2], again[1])
    for k in range(0, groups, 2):
        averages[k + 1] = swapped(averages[k], "replica", 1)
    here = [k for k in range(groups) if k % 2 == 0]
    late = [k for k in range(groups) if k not in here]
    outs = update(count, here, [averages[k] for k in here], squares, params, momentum)
    if late:
        outs = update(
            count, late, [averages[k] for k in late], squares, params, momentum, outs
        )
    return outs


def solution(mesh):
    placed = (P("replica", "fsdp", None), P("fsdp", None), P("fsdp", None))
    return jax.shard_map(
        per_device,
        mesh=mesh,
        in_specs=placed,
        out_specs=(P("fsdp", None), P("fsdp", None)),
        check_vma=False,
    )
```

```python
import functools

import jax
import jax.numpy as jnp
from jax import lax
from jax.experimental import pallas as pl
from jax.experimental.pallas import tpu as pltpu
from jax.sharding import PartitionSpec as P

WIDE = jnp.float32
VMEM = pl.BlockSpec(memory_space=pltpu.VMEM)
HBM = pl.BlockSpec(memory_space=pltpu.HBM)
LIMIT = 16 * 1024 * 1024


def swapped(value, axis, flip):
    size = lax.axis_size(axis)
    return lax.ppermute(value, axis, [(i, i ^ flip) for i in range(size)])


def piece_of(k, width):
    return pl.ds(pl.multiple_of((lax.axis_index("replica") ^ k) * width, width), width)


def tree(parts):
    while len(parts) > 1:
        parts = [parts[i] + parts[i + 1] for i in range(0, len(parts), 2)]
    return parts[0]


def cut_kernel(flips, arrays, *refs):
    grad, sems = refs[0], refs[-1]
    outs = refs[1 + arrays : -1]
    moves = [(grad.at[0, :, piece_of(k, outs[0].shape[1])], out) for k, out in zip(flips, outs)]
    moves += list(zip(refs[1 : 1 + arrays], outs[len(flips) :]))
    copies = [
        pltpu.make_async_copy(source, out, sems.at[i])
        for i, (source, out) in enumerate(moves)
    ]
    for copy in copies:
        copy.start()
    for copy in copies:
        copy.wait()


def cut(grad, width, flips, *arrays):
    piece = jax.ShapeDtypeStruct((grad.shape[1], width), grad.dtype)
    out_shape = [piece] * len(flips) + [jax.ShapeDtypeStruct(x.shape, x.dtype) for x in arrays]
    held = [pltpu.with_memory_space_constraint(x, pltpu.HBM) for x in (grad, *arrays)]
    outs = pl.pallas_call(
        functools.partial(cut_kernel, flips, len(arrays)),
        out_shape=out_shape,
        in_specs=[HBM] * len(held),
        out_specs=[VMEM] * len(out_shape),
        scratch_shapes=[pltpu.SemaphoreType.DMA((len(out_shape),))],
        compiler_params=pltpu.CompilerParams(vmem_limit_bytes=LIMIT),
    )(*held)
    return dict(zip(flips, outs)), outs[len(flips) :]


def average_kernel(groups, *refs):
    pieces, rest = refs[:groups], refs[groups:]
    if len(rest) > 2:
        first, second, average, squares, other_sum = rest
        other_sum[...] = first[...].astype(WIDE) + second[...].astype(WIDE)
    else:
        average, squares = rest
    mean = tree([piece[...].astype(WIDE) for piece in pieces]) / WIDE(groups)
    average[...] = mean
    row = jnp.sum(mean * mean, axis=0, keepdims=True)
    lanes = functools.reduce(
        jnp.add, [row[:, i : i + 128] for i in range(0, row.shape[1], 128)]
    )
    squares[...] = jnp.broadcast_to(lanes[None], squares.shape)


def join_kernel(groups, here, first, second, average):
    there = first[...].astype(WIDE) + second[...].astype(WIDE)
    average[...] = (here[...] + there) / WIDE(groups)


def update_kernel(count, flips, passed, squares, params, momentum, *refs):
    averages, refs = refs[: len(flips)], refs[len(flips) + passed :]
    new_params, new_momentum, params_out, momentum_out, sems = refs
    square_sum = jnp.sum(squares[...], keepdims=True).reshape(1, 1)
    factor = 0.2 / jnp.sqrt(square_sum / WIDE(count) + 1e-06)
    width = averages[0].shape[1]
    copies = []
    for i, (k, average) in enumerate(zip(flips, averages)):
        cols = piece_of(k, width)
        clipped = factor * average[...]
        fresh = 0.9 * momentum[:, cols] + clipped
        momentum_out[i] = fresh
        params_out[i] = params[:, cols] - 0.7 * (clipped + 0.9 * fresh)
        copies += [
            pltpu.make_async_copy(momentum_out.at[i], new_momentum.at[:, cols], sems.at[0, i]),
            pltpu.make_async_copy(params_out.at[i], new_params.at[:, cols], sems.at[1, i]),
        ]
        copies[-2].start()
        copies[-1].start()
    for copy in copies:
        copy.wait()


def update(count, flips, averages, squares, params, momentum, earlier=()):
    rows, width = averages[0].shape
    out = jax.ShapeDtypeStruct(params.shape, WIDE)
    first = 3 + len(flips)
    return pl.pallas_call(
        functools.partial(update_kernel, count, flips, len(earlier)),
        out_shape=[out, out],
        in_specs=[VMEM] * first + [HBM] * len(earlier),
        out_specs=[HBM] * 2,
        scratch_shapes=[
            pltpu.VMEM((len(flips), rows, width), WIDE),
            pltpu.VMEM((len(flips), rows, width), WIDE),
            pltpu.SemaphoreType.DMA((2, len(flips))),
        ],
        input_output_aliases={first + i: i for i in range(len(earlier))},
        compiler_params=pltpu.CompilerParams(vmem_limit_bytes=LIMIT),
    )(squares, params, momentum, *averages, *earlier)


def per_device(pseudo_grad, params, momentum):
    groups = lax.axis_size("replica")
    devices = groups * lax.axis_size("fsdp")
    rows, columns = params.shape
    width = columns // groups
    count = rows * lax.axis_size("fsdp") * columns
    limit = pltpu.CompilerParams(vmem_limit_bytes=LIMIT)
    pieces, _ = cut(pseudo_grad, width, range(2, groups))
    pieces, pseudo_grad, params, momentum = lax.optimization_barrier(
        (pieces, pseudo_grad, params, momentum)
    )
    moved = {k: swapped(pieces[k], "replica", k) for k in range(2, groups)}
    near, (params,) = cut(pseudo_grad, width, range(2), params)
    moved.update({0: near[0], 1: swapped(near[1], "replica", 1)})
    again = {}
    if groups == 4:
        near, params, momentum = lax.optimization_barrier((near, params, momentum))
        _, (momentum,) = cut(pseudo_grad, width, (), momentum)
        near, params, momentum = lax.optimization_barrier((near, params, momentum))
        again = {k: swapped(near[k ^ 2], "replica", k) for k in (2, 3)}
        again[1] = swapped(pieces[3], "replica", 1)
    else:
        _, (momentum,) = cut(pseudo_grad, width, (), momentum)
    wide_piece = jax.ShapeDtypeStruct((rows, width), WIDE)
    parts = [moved[k] for k in range(groups)]
    out_shape = [wide_piece, jax.ShapeDtypeStruct((devices, 1, 128), WIDE)]
    if groups == 4:
        parts += [pieces[2], again.pop(1)]
        out_shape += [wide_piece]
    average, squares, *other_sum = pl.pallas_call(
        functools.partial(average_kernel, groups),
        out_shape=out_shape,
        in_specs=[VMEM] * len(parts),
        out_specs=[VMEM] * len(out_shape),
        compiler_params=limit,
    )(*parts)
    averages = {0: average}
    if groups != 4:
        averages.update({k: swapped(average, "replica", k) for k in range(2, groups, 2)})
    squares = lax.all_to_all(
        squares, ("replica", "fsdp"), split_axis=0, concat_axis=0, tiled=True
    )
    squares, again = lax.optimization_barrier((squares, again))
    if groups == 4:
        averages[2] = pl.pallas_call(
            functools.partial(join_kernel, groups),
            out_shape=wide_piece,
            in_specs=[VMEM] * 3,
            out_specs=VMEM,
            compiler_params=limit,
        )(*other_sum, again[2], again[3])
    squares, averages = lax.optimization_barrier((squares, averages))
    for k in range(0, groups, 2):
        averages[k + 1] = swapped(averages[k], "replica", 1)
    here = [k for k in range(groups) if k % 2 == 0]
    late = [k for k in range(groups) if k not in here]
    outs = update(count, here, [averages[k] for k in here], squares, params, momentum)
    if late:
        outs = update(
            count, late, [averages[k] for k in late], squares, params, momentum, outs
        )
    return outs


def solution(mesh):
    placed = (P("replica", "fsdp", None), P("fsdp", None), P("fsdp", None))
    return jax.shard_map(
        per_device,
        mesh=mesh,
        in_specs=placed,
        out_specs=(P("fsdp", None), P("fsdp", None)),
        check_vma=False,
    )
```

```python
import functools

import jax
import jax.numpy as jnp
from jax import lax
from jax.experimental import pallas as pl
from jax.experimental.pallas import tpu as pltpu
from jax.sharding import PartitionSpec as P

WIDE = jnp.float32
VMEM = pl.BlockSpec(memory_space=pltpu.VMEM)
HBM = pl.BlockSpec(memory_space=pltpu.HBM)
LIMIT = 16 * 1024 * 1024


def swapped(value, axis, flip):
    size = lax.axis_size(axis)
    return lax.ppermute(value, axis, [(i, i ^ flip) for i in range(size)])


def piece_of(k, width):
    return pl.ds(pl.multiple_of((lax.axis_index("replica") ^ k) * width, width), width)


def tree(parts):
    while len(parts) > 1:
        parts = [parts[i] + parts[i + 1] for i in range(0, len(parts), 2)]
    return parts[0]


def cut_kernel(flips, arrays, *refs):
    grad, sems = refs[0], refs[-1]
    outs = refs[1 + arrays : -1]
    moves = [(grad.at[0, :, piece_of(k, outs[0].shape[1])], out) for k, out in zip(flips, outs)]
    moves += list(zip(refs[1 : 1 + arrays], outs[len(flips) :]))
    copies = [
        pltpu.make_async_copy(source, out, sems.at[i])
        for i, (source, out) in enumerate(moves)
    ]
    for copy in copies:
        copy.start()
    for copy in copies:
        copy.wait()


def cut(grad, width, flips, *arrays):
    piece = jax.ShapeDtypeStruct((grad.shape[1], width), grad.dtype)
    out_shape = [piece] * len(flips) + [jax.ShapeDtypeStruct(x.shape, x.dtype) for x in arrays]
    held = [pltpu.with_memory_space_constraint(x, pltpu.HBM) for x in (grad, *arrays)]
    outs = pl.pallas_call(
        functools.partial(cut_kernel, flips, len(arrays)),
        out_shape=out_shape,
        in_specs=[HBM] * len(held),
        out_specs=[VMEM] * len(out_shape),
        scratch_shapes=[pltpu.SemaphoreType.DMA((len(out_shape),))],
        compiler_params=pltpu.CompilerParams(vmem_limit_bytes=LIMIT),
    )(*held)
    return dict(zip(flips, outs)), outs[len(flips) :]


def average_kernel(groups, *refs):
    pieces, rest = refs[:groups], refs[groups:]
    if len(rest) > 2:
        first, second, average, squares, other_sum = rest
        other_sum[...] = first[...].astype(WIDE) + second[...].astype(WIDE)
    else:
        average, squares = rest
    mean = tree([piece[...].astype(WIDE) for piece in pieces]) / WIDE(groups)
    average[...] = mean
    row = jnp.sum(mean * mean, axis=0, keepdims=True)
    lanes = functools.reduce(
        jnp.add, [row[:, i : i + 128] for i in range(0, row.shape[1], 128)]
    )
    squares[...] = jnp.broadcast_to(lanes[None], squares.shape)


def join_kernel(groups, here, first, second, average):
    there = first[...].astype(WIDE) + second[...].astype(WIDE)
    average[...] = (here[...] + there) / WIDE(groups)


def factor_kernel(count, squares, factor):
    square_sum = jnp.sum(squares[...], keepdims=True).reshape(1, 1)
    factor[...] = jnp.broadcast_to(0.2 / jnp.sqrt(square_sum / WIDE(count) + 1e-06), factor.shape)


def update_kernel(flips, passed, factor, params, momentum, *refs):
    averages, refs = refs[: len(flips)], refs[len(flips) + passed :]
    new_params, new_momentum, params_out, momentum_out, sems = refs
    width = averages[0].shape[1]
    copies = []
    for i, (k, average) in enumerate(zip(flips, averages)):
        cols = piece_of(k, width)
        clipped = factor[:, :1] * average[...]
        fresh = 0.9 * momentum[:, cols] + clipped
        momentum_out[i] = fresh
        params_out[i] = params[:, cols] - 0.7 * (clipped + 0.9 * fresh)
        copies += [
            pltpu.make_async_copy(momentum_out.at[i], new_momentum.at[:, cols], sems.at[0, i]),
            pltpu.make_async_copy(params_out.at[i], new_params.at[:, cols], sems.at[1, i]),
        ]
        copies[-2].start()
        copies[-1].start()
    for copy in copies:
        copy.wait()


def update(flips, averages, factor, params, momentum, earlier=()):
    rows, width = averages[0].shape
    out = jax.ShapeDtypeStruct(params.shape, WIDE)
    first = 3 + len(flips)
    return pl.pallas_call(
        functools.partial(update_kernel, flips, len(earlier)),
        out_shape=[out, out],
        in_specs=[VMEM] * first + [HBM] * len(earlier),
        out_specs=[HBM] * 2,
        scratch_shapes=[
            pltpu.VMEM((len(flips), rows, width), WIDE),
            pltpu.VMEM((len(flips), rows, width), WIDE),
            pltpu.SemaphoreType.DMA((2, len(flips))),
        ],
        input_output_aliases={first + i: i for i in range(len(earlier))},
        compiler_params=pltpu.CompilerParams(vmem_limit_bytes=LIMIT),
    )(factor, params, momentum, *averages, *earlier)


def per_device(pseudo_grad, params, momentum):
    groups = lax.axis_size("replica")
    devices = groups * lax.axis_size("fsdp")
    rows, columns = params.shape
    width = columns // groups
    count = rows * lax.axis_size("fsdp") * columns
    limit = pltpu.CompilerParams(vmem_limit_bytes=LIMIT)
    pieces, _ = cut(pseudo_grad, width, range(2, groups))
    pieces, pseudo_grad, params, momentum = lax.optimization_barrier(
        (pieces, pseudo_grad, params, momentum)
    )
    moved = {k: swapped(pieces[k], "replica", k) for k in range(2, groups)}
    near, (params,) = cut(pseudo_grad, width, range(2), params)
    moved.update({0: near[0], 1: swapped(near[1], "replica", 1)})
    again = {}
    if groups == 4:
        near, params, momentum = lax.optimization_barrier((near, params, momentum))
        _, (momentum,) = cut(pseudo_grad, width, (), momentum)
        near, params, momentum = lax.optimization_barrier((near, params, momentum))
        again = {k: swapped(near[k ^ 2], "replica", k) for k in (2, 3)}
        again[1] = swapped(pieces[3], "replica", 1)
    else:
        _, (momentum,) = cut(pseudo_grad, width, (), momentum)
    wide_piece = jax.ShapeDtypeStruct((rows, width), WIDE)
    parts = [moved[k] for k in range(groups)]
    out_shape = [wide_piece, jax.ShapeDtypeStruct((devices, 1, 128), WIDE)]
    if groups == 4:
        parts += [pieces[2], again.pop(1)]
        out_shape += [wide_piece]
    average, squares, *other_sum = pl.pallas_call(
        functools.partial(average_kernel, groups),
        out_shape=out_shape,
        in_specs=[VMEM] * len(parts),
        out_specs=[VMEM] * len(out_shape),
        compiler_params=limit,
    )(*parts)
    averages = {0: average}
    if groups != 4:
        averages.update({k: swapped(average, "replica", k) for k in range(2, groups, 2)})
    squares = lax.all_to_all(
        squares, ("replica", "fsdp"), split_axis=0, concat_axis=0, tiled=True
    )
    factor = pl.pallas_call(
        functools.partial(factor_kernel, count),
        out_shape=jax.ShapeDtypeStruct((1, 128), WIDE),
        in_specs=[VMEM],
        out_specs=VMEM,
        compiler_params=limit,
    )(squares)
    factor, again = lax.optimization_barrier((factor, again))
    if groups == 4:
        averages[2] = pl.pallas_call(
            functools.partial(join_kernel, groups),
            out_shape=wide_piece,
            in_specs=[VMEM] * 3,
            out_specs=VMEM,
            compiler_params=limit,
        )(*other_sum, again[2], again[3])
    factor, averages = lax.optimization_barrier((factor, averages))
    for k in range(0, groups, 2):
        averages[k + 1] = swapped(averages[k], "replica", 1)
    here = [k for k in range(groups) if k % 2 == 0]
    late = [k for k in range(groups) if k not in here]
    outs = update(here, [averages[k] for k in here], factor, params, momentum)
    if late:
        outs = update(
            late, [averages[k] for k in late], factor, params, momentum, outs
        )
    return outs


def solution(mesh):
    placed = (P("replica", "fsdp", None), P("fsdp", None), P("fsdp", None))
    return jax.shard_map(
        per_device,
        mesh=mesh,
        in_specs=placed,
        out_specs=(P("fsdp", None), P("fsdp", None)),
        check_vma=False,
    )
```

```python
import functools

import jax
import jax.numpy as jnp
from jax import lax
from jax.experimental import pallas as pl
from jax.experimental.pallas import tpu as pltpu
from jax.sharding import PartitionSpec as P

WIDE = jnp.float32
VMEM = pl.BlockSpec(memory_space=pltpu.VMEM)
HBM = pl.BlockSpec(memory_space=pltpu.HBM)
LIMIT = 16 * 1024 * 1024


def swapped(value, axis, flip):
    size = lax.axis_size(axis)
    return lax.ppermute(value, axis, [(i, i ^ flip) for i in range(size)])


def piece_of(k, width):
    return pl.ds(pl.multiple_of((lax.axis_index("replica") ^ k) * width, width), width)


def tree(parts):
    while len(parts) > 1:
        parts = [parts[i] + parts[i + 1] for i in range(0, len(parts), 2)]
    return parts[0]


def cut_kernel(flips, arrays, *refs):
    grad, sems = refs[0], refs[-1]
    outs = refs[1 + arrays : -1]
    moves = [(grad.at[0, :, piece_of(k, outs[0].shape[1])], out) for k, out in zip(flips, outs)]
    moves += list(zip(refs[1 : 1 + arrays], outs[len(flips) :]))
    copies = [
        pltpu.make_async_copy(source, out, sems.at[i])
        for i, (source, out) in enumerate(moves)
    ]
    for copy in copies:
        copy.start()
    for copy in copies:
        copy.wait()


def cut(grad, width, flips, *arrays):
    piece = jax.ShapeDtypeStruct((grad.shape[1], width), grad.dtype)
    out_shape = [piece] * len(flips) + [jax.ShapeDtypeStruct(x.shape, x.dtype) for x in arrays]
    held = [pltpu.with_memory_space_constraint(x, pltpu.HBM) for x in (grad, *arrays)]
    outs = pl.pallas_call(
        functools.partial(cut_kernel, flips, len(arrays)),
        out_shape=out_shape,
        in_specs=[HBM] * len(held),
        out_specs=[VMEM] * len(out_shape),
        scratch_shapes=[pltpu.SemaphoreType.DMA((len(out_shape),))],
        compiler_params=pltpu.CompilerParams(vmem_limit_bytes=LIMIT),
    )(*held)
    return dict(zip(flips, outs)), outs[len(flips) :]


def average_kernel(groups, *refs):
    pieces, rest = refs[:groups], refs[groups:]
    if len(rest) > 3:
        first, second, *average, squares, other_sum = rest
        other_sum[...] = first[...].astype(WIDE) + second[...].astype(WIDE)
    else:
        *average, squares = rest
    mean = tree([piece[...].astype(WIDE) for piece in pieces]) / WIDE(groups)
    for i, half in enumerate(average):
        half[...] = mean[i * half.shape[0] : (i + 1) * half.shape[0]]
    row = jnp.sum(mean * mean, axis=0, keepdims=True)
    lanes = functools.reduce(
        jnp.add, [row[:, i : i + 128] for i in range(0, row.shape[1], 128)]
    )
    squares[...] = jnp.broadcast_to(lanes[None], squares.shape)


def join_kernel(groups, here, first, second, average):
    there = first[...].astype(WIDE) + second[...].astype(WIDE)
    average[...] = (here[...] + there) / WIDE(groups)


def factor_kernel(count, squares, factor):
    square_sum = jnp.sum(squares[...], keepdims=True).reshape(1, 1)
    factor[...] = jnp.broadcast_to(0.2 / jnp.sqrt(square_sum / WIDE(count) + 1e-06), factor.shape)


def update_kernel(flips, sizes, passed, factor, params, momentum, *refs):
    averages = []
    for size in sizes:
        averages.append(jnp.concatenate([ref[...] for ref in refs[:size]]))
        refs = refs[size:]
    refs = refs[passed:]
    new_params, new_momentum, params_out, momentum_out, sems = refs
    width = params_out.shape[2]
    copies = []
    for i, (k, average) in enumerate(zip(flips, averages)):
        cols = piece_of(k, width)
        clipped = factor[:, :1] * average
        fresh = 0.9 * momentum[:, cols] + clipped
        momentum_out[i] = fresh
        params_out[i] = params[:, cols] - 0.7 * (clipped + 0.9 * fresh)
        copies += [
            pltpu.make_async_copy(momentum_out.at[i], new_momentum.at[:, cols], sems.at[0, i]),
            pltpu.make_async_copy(params_out.at[i], new_params.at[:, cols], sems.at[1, i]),
        ]
        copies[-2].start()
        copies[-1].start()
    for copy in copies:
        copy.wait()


def update(flips, averages, factor, params, momentum, earlier=()):
    sizes = [len(average) for average in averages]
    parts = [part for average in averages for part in average]
    rows, width = params.shape[0], parts[0].shape[1]
    out = jax.ShapeDtypeStruct(params.shape, WIDE)
    first = 3 + len(parts)
    return pl.pallas_call(
        functools.partial(update_kernel, flips, sizes, len(earlier)),
        out_shape=[out, out],
        in_specs=[VMEM] * first + [HBM] * len(earlier),
        out_specs=[HBM] * 2,
        scratch_shapes=[
            pltpu.VMEM((len(flips), rows, width), WIDE),
            pltpu.VMEM((len(flips), rows, width), WIDE),
            pltpu.SemaphoreType.DMA((2, len(flips))),
        ],
        input_output_aliases={first + i: i for i in range(len(earlier))},
        compiler_params=pltpu.CompilerParams(vmem_limit_bytes=LIMIT),
    )(factor, params, momentum, *parts, *earlier)


def per_device(pseudo_grad, params, momentum):
    groups = lax.axis_size("replica")
    devices = groups * lax.axis_size("fsdp")
    rows, columns = params.shape
    width = columns // groups
    count = rows * lax.axis_size("fsdp") * columns
    limit = pltpu.CompilerParams(vmem_limit_bytes=LIMIT)
    pieces, _ = cut(pseudo_grad, width, range(2, groups))
    pieces, pseudo_grad, params, momentum = lax.optimization_barrier(
        (pieces, pseudo_grad, params, momentum)
    )
    moved = {k: swapped(pieces[k], "replica", k) for k in range(2, groups)}
    near, (params,) = cut(pseudo_grad, width, range(2), params)
    moved.update({0: near[0], 1: swapped(near[1], "replica", 1)})
    again = {}
    if groups == 4:
        near, params, momentum = lax.optimization_barrier((near, params, momentum))
        _, (momentum,) = cut(pseudo_grad, width, (), momentum)
        near, params, momentum = lax.optimization_barrier((near, params, momentum))
        again = {k: swapped(near[k ^ 2], "replica", k) for k in (2, 3)}
        again[1] = swapped(pieces[3], "replica", 1)
    else:
        _, (momentum,) = cut(pseudo_grad, width, (), momentum)
    wide_piece = jax.ShapeDtypeStruct((rows, width), WIDE)
    parts = [moved[k] for k in range(groups)]
    half_piece = jax.ShapeDtypeStruct((rows // 2, width), WIDE)
    out_shape = [half_piece] * 2 + [jax.ShapeDtypeStruct((devices, 1, 128), WIDE)]
    if groups == 4:
        parts += [pieces[2], again.pop(1)]
        out_shape += [wide_piece]
    low, high, squares, *other_sum = pl.pallas_call(
        functools.partial(average_kernel, groups),
        out_shape=out_shape,
        in_specs=[VMEM] * len(parts),
        out_specs=[VMEM] * len(out_shape),
        compiler_params=limit,
    )(*parts)
    averages = {0: [low, high], 1: [swapped(x, "replica", 1) for x in (low, high)]}
    if groups != 4:
        for k in range(2, groups, 2):
            averages[k] = [swapped(x, "replica", k) for x in (low, high)]
    squares = lax.all_to_all(
        squares, ("replica", "fsdp"), split_axis=0, concat_axis=0, tiled=True
    )
    factor = pl.pallas_call(
        functools.partial(factor_kernel, count),
        out_shape=jax.ShapeDtypeStruct((1, 128), WIDE),
        in_specs=[VMEM],
        out_specs=VMEM,
        compiler_params=limit,
    )(squares)
    factor, again = lax.optimization_barrier((factor, again))
    if groups == 4:
        joined = pl.pallas_call(
            functools.partial(join_kernel, groups),
            out_shape=wide_piece,
            in_specs=[VMEM] * 3,
            out_specs=VMEM,
            compiler_params=limit,
        )(*other_sum, again[2], again[3])
        averages[2] = [joined]
    factor, averages = lax.optimization_barrier((factor, averages))
    for k in range(2, groups, 2):
        averages[k + 1] = [swapped(x, "replica", 1) for x in averages[k]]
    here = [k for k in range(groups) if k < 2 or k % 2 == 0]
    late = [k for k in range(groups) if k not in here]
    outs = update(here, [averages[k] for k in here], factor, params, momentum)
    if late:
        outs = update(
            late, [averages[k] for k in late], factor, params, momentum, outs
        )
    return outs


def solution(mesh):
    placed = (P("replica", "fsdp", None), P("fsdp", None), P("fsdp", None))
    return jax.shard_map(
        per_device,
        mesh=mesh,
        in_specs=placed,
        out_specs=(P("fsdp", None), P("fsdp", None)),
        check_vma=False,
    )
```

```python
import functools

import jax
import jax.numpy as jnp
from jax import lax
from jax.experimental import pallas as pl
from jax.experimental.pallas import tpu as pltpu
from jax.sharding import PartitionSpec as P

WIDE = jnp.float32
VMEM = pl.BlockSpec(memory_space=pltpu.VMEM)
HBM = pl.BlockSpec(memory_space=pltpu.HBM)
LIMIT = 16 * 1024 * 1024


def swapped(value, axis, flip):
    size = lax.axis_size(axis)
    return lax.ppermute(value, axis, [(i, i ^ flip) for i in range(size)])


def piece_of(k, width):
    return pl.ds(pl.multiple_of((lax.axis_index("replica") ^ k) * width, width), width)


def tree(parts):
    while len(parts) > 1:
        parts = [parts[i] + parts[i + 1] for i in range(0, len(parts), 2)]
    return parts[0]


def cut_kernel(flips, arrays, *refs):
    grad, sems = refs[0], refs[-1]
    outs = refs[1 + arrays : -1]
    moves = [(grad.at[0, :, piece_of(k, outs[0].shape[1])], out) for k, out in zip(flips, outs)]
    moves += list(zip(refs[1 : 1 + arrays], outs[len(flips) :]))
    copies = [
        pltpu.make_async_copy(source, out, sems.at[i])
        for i, (source, out) in enumerate(moves)
    ]
    for copy in copies:
        copy.start()
    for copy in copies:
        copy.wait()


def cut(grad, width, flips, *arrays):
    piece = jax.ShapeDtypeStruct((grad.shape[1], width), grad.dtype)
    out_shape = [piece] * len(flips) + [jax.ShapeDtypeStruct(x.shape, x.dtype) for x in arrays]
    held = [pltpu.with_memory_space_constraint(x, pltpu.HBM) for x in (grad, *arrays)]
    outs = pl.pallas_call(
        functools.partial(cut_kernel, flips, len(arrays)),
        out_shape=out_shape,
        in_specs=[HBM] * len(held),
        out_specs=[VMEM] * len(out_shape),
        scratch_shapes=[pltpu.SemaphoreType.DMA((len(out_shape),))],
        compiler_params=pltpu.CompilerParams(vmem_limit_bytes=LIMIT),
    )(*held)
    return dict(zip(flips, outs)), outs[len(flips) :]


def average_kernel(groups, *refs):
    pieces, rest = refs[:groups], refs[groups:]
    if len(rest) > 3:
        first, second, *average, squares, other_sum = rest
        other_sum[...] = first[...].astype(WIDE) + second[...].astype(WIDE)
    else:
        *average, squares = rest
    mean = tree([piece[...].astype(WIDE) for piece in pieces]) / WIDE(groups)
    for i, half in enumerate(average):
        half[...] = mean[i * half.shape[0] : (i + 1) * half.shape[0]]
    row = jnp.sum(mean * mean, axis=0, keepdims=True)
    lanes = functools.reduce(
        jnp.add, [row[:, i : i + 128] for i in range(0, row.shape[1], 128)]
    )
    squares[...] = jnp.broadcast_to(lanes[None], squares.shape)


def join_kernel(groups, here, first, second, average):
    there = first[...].astype(WIDE) + second[...].astype(WIDE)
    average[...] = (here[...] + there) / WIDE(groups)


def factor_kernel(count, squares, factor):
    square_sum = jnp.sum(squares[...], keepdims=True).reshape(1, 1)
    factor[...] = jnp.broadcast_to(0.2 / jnp.sqrt(square_sum / WIDE(count) + 1e-06), factor.shape)


def update_kernel(flips, sizes, passed, factor, params, momentum, *refs):
    averages = []
    for size in sizes:
        averages.append(jnp.concatenate([ref[...] for ref in refs[:size]]))
        refs = refs[size:]
    refs = refs[passed:]
    new_params, new_momentum, params_out, momentum_out, sems = refs
    width = params_out.shape[2]
    copies = []
    for i, (k, average) in enumerate(zip(flips, averages)):
        cols = piece_of(k, width)
        clipped = factor[:, :1] * average
        fresh = 0.9 * momentum[:, cols] + clipped
        momentum_out[i] = fresh
        params_out[i] = params[:, cols] - 0.7 * (clipped + 0.9 * fresh)
        copies += [
            pltpu.make_async_copy(momentum_out.at[i], new_momentum.at[:, cols], sems.at[0, i]),
            pltpu.make_async_copy(params_out.at[i], new_params.at[:, cols], sems.at[1, i]),
        ]
        copies[-2].start()
        copies[-1].start()
    for copy in copies:
        copy.wait()


def update(flips, averages, factor, params, momentum, earlier=()):
    sizes = [len(average) for average in averages]
    parts = [part for average in averages for part in average]
    rows, width = params.shape[0], parts[0].shape[1]
    out = jax.ShapeDtypeStruct(params.shape, WIDE)
    first = 3 + len(parts)
    return pl.pallas_call(
        functools.partial(update_kernel, flips, sizes, len(earlier)),
        out_shape=[out, out],
        in_specs=[VMEM] * first + [HBM] * len(earlier),
        out_specs=[HBM] * 2,
        scratch_shapes=[
            pltpu.VMEM((len(flips), rows, width), WIDE),
            pltpu.VMEM((len(flips), rows, width), WIDE),
            pltpu.SemaphoreType.DMA((2, len(flips))),
        ],
        input_output_aliases={first + i: i for i in range(len(earlier))},
        compiler_params=pltpu.CompilerParams(vmem_limit_bytes=LIMIT),
    )(factor, params, momentum, *parts, *earlier)


def per_device(pseudo_grad, params, momentum):
    groups = lax.axis_size("replica")
    devices = groups * lax.axis_size("fsdp")
    rows, columns = params.shape
    width = columns // groups
    count = rows * lax.axis_size("fsdp") * columns
    limit = pltpu.CompilerParams(vmem_limit_bytes=LIMIT)
    pieces, _ = cut(pseudo_grad, width, range(2, groups))
    pieces, pseudo_grad, params, momentum = lax.optimization_barrier(
        (pieces, pseudo_grad, params, momentum)
    )
    moved = {k: swapped(pieces[k], "replica", k) for k in range(2, groups)}
    near, (params,) = cut(pseudo_grad, width, range(2), params)
    moved.update({0: near[0], 1: swapped(near[1], "replica", 1)})
    again = {}
    if groups == 4:
        near, three, params, momentum = lax.optimization_barrier(
            (near, pieces[3], params, momentum)
        )
        _, (momentum,) = cut(pseudo_grad, width, (), momentum)
        near, params, momentum = lax.optimization_barrier((near, params, momentum))
        again = {k: swapped(near[k ^ 2], "replica", k) for k in (2, 3)}
        again[1] = swapped(three, "replica", 1)
    else:
        _, (momentum,) = cut(pseudo_grad, width, (), momentum)
    wide_piece = jax.ShapeDtypeStruct((rows, width), WIDE)
    parts = [moved[k] for k in range(groups)]
    half_piece = jax.ShapeDtypeStruct((rows // 2, width), WIDE)
    out_shape = [half_piece] * 2 + [jax.ShapeDtypeStruct((devices, 1, 128), WIDE)]
    if groups == 4:
        parts += [pieces[2], again.pop(1)]
        out_shape += [wide_piece]
    low, high, squares, *other_sum = pl.pallas_call(
        functools.partial(average_kernel, groups),
        out_shape=out_shape,
        in_specs=[VMEM] * len(parts),
        out_specs=[VMEM] * len(out_shape),
        compiler_params=limit,
    )(*parts)
    averages = {0: [low, high], 1: [swapped(x, "replica", 1) for x in (low, high)]}
    if groups != 4:
        for k in range(2, groups, 2):
            averages[k] = [swapped(x, "replica", k) for x in (low, high)]
    squares = lax.all_to_all(
        squares, ("replica", "fsdp"), split_axis=0, concat_axis=0, tiled=True
    )
    factor = pl.pallas_call(
        functools.partial(factor_kernel, count),
        out_shape=jax.ShapeDtypeStruct((1, 128), WIDE),
        in_specs=[VMEM],
        out_specs=VMEM,
        compiler_params=limit,
    )(squares)
    factor, again = lax.optimization_barrier((factor, again))
    if groups == 4:
        joined = pl.pallas_call(
            functools.partial(join_kernel, groups),
            out_shape=wide_piece,
            in_specs=[VMEM] * 3,
            out_specs=VMEM,
            compiler_params=limit,
        )(*other_sum, again[2], again[3])
        averages[2] = [joined]
    factor, averages = lax.optimization_barrier((factor, averages))
    for k in range(2, groups, 2):
        averages[k + 1] = [swapped(x, "replica", 1) for x in averages[k]]
    here = [k for k in range(groups) if k < 2 or k % 2 == 0]
    late = [k for k in range(groups) if k not in here]
    outs = update(here, [averages[k] for k in here], factor, params, momentum)
    if late:
        outs = update(
            late, [averages[k] for k in late], factor, params, momentum, outs
        )
    return outs


def solution(mesh):
    placed = (P("replica", "fsdp", None), P("fsdp", None), P("fsdp", None))
    return jax.shard_map(
        per_device,
        mesh=mesh,
        in_specs=placed,
        out_specs=(P("fsdp", None), P("fsdp", None)),
        check_vma=False,
    )
```

```python
import functools

import jax
import jax.numpy as jnp
from jax import lax
from jax.experimental import pallas as pl
from jax.experimental.pallas import tpu as pltpu
from jax.sharding import PartitionSpec as P

WIDE = jnp.float32
VMEM = pl.BlockSpec(memory_space=pltpu.VMEM)
HBM = pl.BlockSpec(memory_space=pltpu.HBM)
LIMIT = 16 * 1024 * 1024


def swapped(value, axis, flip):
    size = lax.axis_size(axis)
    return lax.ppermute(value, axis, [(i, i ^ flip) for i in range(size)])


def piece_of(k, width):
    return pl.ds(pl.multiple_of((lax.axis_index("replica") ^ k) * width, width), width)


def tree(parts):
    while len(parts) > 1:
        parts = [parts[i] + parts[i + 1] for i in range(0, len(parts), 2)]
    return parts[0]


def cut_kernel(flips, arrays, *refs):
    grad, sems = refs[0], refs[-1]
    outs = refs[1 + arrays : -1]
    moves = [(grad.at[0, :, piece_of(k, outs[0].shape[1])], out) for k, out in zip(flips, outs)]
    moves += list(zip(refs[1 : 1 + arrays], outs[len(flips) :]))
    copies = [
        pltpu.make_async_copy(source, out, sems.at[i])
        for i, (source, out) in enumerate(moves)
    ]
    for copy in copies:
        copy.start()
    for copy in copies:
        copy.wait()


def cut(grad, width, flips, *arrays):
    piece = jax.ShapeDtypeStruct((grad.shape[1], width), grad.dtype)
    out_shape = [piece] * len(flips) + [jax.ShapeDtypeStruct(x.shape, x.dtype) for x in arrays]
    held = [pltpu.with_memory_space_constraint(x, pltpu.HBM) for x in (grad, *arrays)]
    outs = pl.pallas_call(
        functools.partial(cut_kernel, flips, len(arrays)),
        out_shape=out_shape,
        in_specs=[HBM] * len(held),
        out_specs=[VMEM] * len(out_shape),
        scratch_shapes=[pltpu.SemaphoreType.DMA((len(out_shape),))],
        compiler_params=pltpu.CompilerParams(vmem_limit_bytes=LIMIT),
    )(*held)
    return dict(zip(flips, outs)), outs[len(flips) :]


def average_kernel(*refs):
    pieces, (average, squares) = refs[:-2], refs[-2:]
    total = tree([piece[...].astype(WIDE) for piece in pieces])
    mean = total / WIDE(len(pieces))
    average[...] = mean
    row = jnp.sum(mean * mean, axis=0, keepdims=True)
    lanes = functools.reduce(
        jnp.add, [row[:, i : i + 128] for i in range(0, row.shape[1], 128)]
    )
    squares[...] = jnp.broadcast_to(lanes[None], squares.shape)


def update_kernel(count, flips, passed, scale, params, momentum, *refs):
    averages, refs = refs[: len(flips)], refs[len(flips) + passed :]
    new_params, new_momentum, factor_out, params_out, momentum_out, sems = refs
    if passed:
        factor = scale[:, :1]
    else:
        square_sum = jnp.sum(scale[...], keepdims=True).reshape(1, 1)
        factor = 0.2 / jnp.sqrt(square_sum / WIDE(count) + 1e-06)
    factor_out[...] = jnp.broadcast_to(factor, factor_out.shape)
    width = averages[0].shape[1]
    copies = []
    for i, (k, average) in enumerate(zip(flips, averages)):
        cols = piece_of(k, width)
        clipped = factor * average[...]
        fresh = 0.9 * momentum[:, cols] + clipped
        momentum_out[i] = fresh
        params_out[i] = params[:, cols] - 0.7 * (clipped + 0.9 * fresh)
        copies += [
            pltpu.make_async_copy(momentum_out.at[i], new_momentum.at[:, cols], sems.at[0, i]),
            pltpu.make_async_copy(params_out.at[i], new_params.at[:, cols], sems.at[1, i]),
        ]
        copies[-2].start()
        copies[-1].start()
    for copy in copies:
        copy.wait()


def update(count, flips, averages, scale, params, momentum, earlier=()):
    rows, width = averages[0].shape
    out = jax.ShapeDtypeStruct(params.shape, WIDE)
    first = 3 + len(flips)
    return pl.pallas_call(
        functools.partial(update_kernel, count, flips, len(earlier)),
        out_shape=[out, out, jax.ShapeDtypeStruct((1, 128), WIDE)],
        in_specs=[VMEM] * first + [HBM] * len(earlier),
        out_specs=[HBM, HBM, VMEM],
        scratch_shapes=[
            pltpu.VMEM((len(flips), rows, width), WIDE),
            pltpu.VMEM((len(flips), rows, width), WIDE),
            pltpu.SemaphoreType.DMA((2, len(flips))),
        ],
        input_output_aliases={first + i: i for i in range(len(earlier))},
        compiler_params=pltpu.CompilerParams(vmem_limit_bytes=LIMIT),
    )(scale, params, momentum, *averages, *earlier)


def per_device(pseudo_grad, params, momentum):
    groups = lax.axis_size("replica")
    devices = groups * lax.axis_size("fsdp")
    rows, columns = params.shape
    width = columns // groups
    count = rows * lax.axis_size("fsdp") * columns
    limit = pltpu.CompilerParams(vmem_limit_bytes=LIMIT)
    pieces, _ = cut(pseudo_grad, width, range(2, groups))
    pieces, pseudo_grad, params, momentum = lax.optimization_barrier(
        (pieces, pseudo_grad, params, momentum)
    )
    moved = {k: swapped(pieces[k], "replica", k) for k in range(2, groups)}
    near, (params, momentum) = cut(pseudo_grad, width, range(2), params, momentum)
    moved.update({0: near[0], 1: swapped(near[1], "replica", 1)})
    average, squares = pl.pallas_call(
        average_kernel,
        out_shape=[
            jax.ShapeDtypeStruct((rows, width), WIDE),
            jax.ShapeDtypeStruct((devices, 1, 128), WIDE),
        ],
        in_specs=[VMEM] * groups,
        out_specs=[VMEM] * 2,
        compiler_params=limit,
    )(*[moved[k] for k in range(groups)])
    averages = {0: average}
    for k in range(2, groups, 2):
        averages[k] = swapped(average, "replica", k)
    averages[1] = swapped(average, "replica", 1)
    squares = lax.all_to_all(
        squares, ("replica", "fsdp"), split_axis=0, concat_axis=0, tiled=True
    )
    squares, averages = lax.optimization_barrier((squares, averages))
    for k in range(2, groups, 2):
        averages[k + 1] = swapped(averages[k], "replica", 1)
    here = [k for k in range(groups) if k < 2 or k % 2 == 0]
    late = [k for k in range(groups) if k not in here]
    *outs, factor = update(
        count, here, [averages[k] for k in here], squares, params, momentum
    )
    if late:
        *outs, factor = update(
            count, late, [averages[k] for k in late], factor, params, momentum, outs
        )
    return tuple(outs)


def solution(mesh):
    placed = (P("replica", "fsdp", None), P("fsdp", None), P("fsdp", None))
    return jax.shard_map(
        per_device,
        mesh=mesh,
        in_specs=placed,
        out_specs=(P("fsdp", None), P("fsdp", None)),
        check_vma=False,
    )
```

```python
import functools

import jax
import jax.numpy as jnp
from jax import lax
from jax.experimental import pallas as pl
from jax.experimental.pallas import tpu as pltpu
from jax.sharding import PartitionSpec as P

WIDE = jnp.float32
VMEM = pl.BlockSpec(memory_space=pltpu.VMEM)
HBM = pl.BlockSpec(memory_space=pltpu.HBM)
LIMIT = 16 * 1024 * 1024


def swapped(value, axis, flip):
    size = lax.axis_size(axis)
    return lax.ppermute(value, axis, [(i, i ^ flip) for i in range(size)])


def piece_of(k, width):
    return pl.ds(pl.multiple_of((lax.axis_index("replica") ^ k) * width, width), width)


def tree(parts):
    while len(parts) > 1:
        parts = [parts[i] + parts[i + 1] for i in range(0, len(parts), 2)]
    return parts[0]


def cut_kernel(flips, arrays, *refs):
    grad, sems = refs[0], refs[-1]
    outs = refs[1 + arrays : -1]
    moves = [(grad.at[0, :, piece_of(k, outs[0].shape[1])], out) for k, out in zip(flips, outs)]
    moves += list(zip(refs[1 : 1 + arrays], outs[len(flips) :]))
    copies = [
        pltpu.make_async_copy(source, out, sems.at[i])
        for i, (source, out) in enumerate(moves)
    ]
    for copy in copies:
        copy.start()
    for copy in copies:
        copy.wait()


def cut(grad, width, flips, *arrays):
    piece = jax.ShapeDtypeStruct((grad.shape[1], width), grad.dtype)
    out_shape = [piece] * len(flips) + [jax.ShapeDtypeStruct(x.shape, x.dtype) for x in arrays]
    held = [pltpu.with_memory_space_constraint(x, pltpu.HBM) for x in (grad, *arrays)]
    outs = pl.pallas_call(
        functools.partial(cut_kernel, flips, len(arrays)),
        out_shape=out_shape,
        in_specs=[HBM] * len(held),
        out_specs=[VMEM] * len(out_shape),
        scratch_shapes=[pltpu.SemaphoreType.DMA((len(out_shape),))],
        compiler_params=pltpu.CompilerParams(vmem_limit_bytes=LIMIT),
    )(*held)
    return dict(zip(flips, outs)), outs[len(flips) :]


def average_kernel(*refs):
    pieces, (average, squares) = refs[:-2], refs[-2:]
    total = tree([piece[...].astype(WIDE) for piece in pieces])
    mean = total / WIDE(len(pieces))
    average[...] = mean
    row = jnp.sum(mean * mean, axis=0, keepdims=True)
    lanes = functools.reduce(
        jnp.add, [row[:, i : i + 128] for i in range(0, row.shape[1], 128)]
    )
    squares[...] = jnp.broadcast_to(lanes[None], squares.shape)


def update_kernel(count, flips, passed, squares, params, momentum, *refs):
    averages, refs = refs[: len(flips)], refs[len(flips) + passed :]
    new_params, new_momentum, params_out, momentum_out, sems = refs
    square_sum = jnp.sum(squares[...], keepdims=True).reshape(1, 1)
    factor = 0.2 / jnp.sqrt(square_sum / WIDE(count) + 1e-06)
    width = averages[0].shape[1]
    copies = []
    for i, (k, average) in enumerate(zip(flips, averages)):
        cols = piece_of(k, width)
        clipped = factor * average[...]
        fresh = 0.9 * momentum[:, cols] + clipped
        momentum_out[i] = fresh
        params_out[i] = params[:, cols] - 0.7 * (clipped + 0.9 * fresh)
        copies += [
            pltpu.make_async_copy(momentum_out.at[i], new_momentum.at[:, cols], sems.at[0, i]),
            pltpu.make_async_copy(params_out.at[i], new_params.at[:, cols], sems.at[1, i]),
        ]
        copies[-2].start()
        copies[-1].start()
    for copy in copies:
        copy.wait()


def update(count, flips, averages, squares, params, momentum, earlier=()):
    rows, width = averages[0].shape
    out = jax.ShapeDtypeStruct(params.shape, WIDE)
    first = 3 + len(flips)
    return pl.pallas_call(
        functools.partial(update_kernel, count, flips, len(earlier)),
        out_shape=[out, out],
        in_specs=[VMEM] * first + [HBM] * len(earlier),
        out_specs=[HBM] * 2,
        scratch_shapes=[
            pltpu.VMEM((len(flips), rows, width), WIDE),
            pltpu.VMEM((len(flips), rows, width), WIDE),
            pltpu.SemaphoreType.DMA((2, len(flips))),
        ],
        input_output_aliases={first + i: i for i in range(len(earlier))},
        compiler_params=pltpu.CompilerParams(vmem_limit_bytes=LIMIT),
    )(squares, params, momentum, *averages, *earlier)


def per_device(pseudo_grad, params, momentum):
    groups = lax.axis_size("replica")
    devices = groups * lax.axis_size("fsdp")
    rows, columns = params.shape
    width = columns // groups
    count = rows * lax.axis_size("fsdp") * columns
    limit = pltpu.CompilerParams(vmem_limit_bytes=LIMIT)
    pieces, _ = cut(pseudo_grad, width, range(2, groups))
    pieces, pseudo_grad, params, momentum = lax.optimization_barrier(
        (pieces, pseudo_grad, params, momentum)
    )
    moved = {k: swapped(pieces[k], "replica", k) for k in reversed(range(2, groups))}
    near, (params, momentum) = cut(pseudo_grad, width, range(2), params, momentum)
    moved.update({0: near[0], 1: swapped(near[1], "replica", 1)})
    average, squares = pl.pallas_call(
        average_kernel,
        out_shape=[
            jax.ShapeDtypeStruct((rows, width), WIDE),
            jax.ShapeDtypeStruct((devices, 1, 128), WIDE),
        ],
        in_specs=[VMEM] * groups,
        out_specs=[VMEM] * 2,
        compiler_params=limit,
    )(*[moved[k] for k in reversed(range(groups))])
    averages = {0: average}
    for k in range(2, groups, 2):
        averages[k] = swapped(average, "replica", k)
    averages[1] = swapped(average, "replica", 1)
    squares = lax.all_to_all(
        squares, ("replica", "fsdp"), split_axis=0, concat_axis=0, tiled=True
    )
    squares, averages = lax.optimization_barrier((squares, averages))
    for k in range(2, groups, 2):
        averages[k + 1] = swapped(averages[k], "replica", 1)
    here = [k for k in range(groups) if k < 2 or k % 2 == 0]
    late = [k for k in range(groups) if k not in here]
    outs = update(count, here, [averages[k] for k in here], squares, params, momentum)
    if late:
        outs = update(
            count, late, [averages[k] for k in late], squares, params, momentum, outs
        )
    return outs


def solution(mesh):
    placed = (P("replica", "fsdp", None), P("fsdp", None), P("fsdp", None))
    return jax.shard_map(
        per_device,
        mesh=mesh,
        in_specs=placed,
        out_specs=(P("fsdp", None), P("fsdp", None)),
        check_vma=False,
    )
```

```python
import functools

import jax
import jax.numpy as jnp
from jax import lax
from jax.experimental import pallas as pl
from jax.experimental.pallas import tpu as pltpu
from jax.sharding import PartitionSpec as P

WIDE = jnp.float32
VMEM = pl.BlockSpec(memory_space=pltpu.VMEM)
HBM = pl.BlockSpec(memory_space=pltpu.HBM)
LIMIT = 16 * 1024 * 1024


def swapped(value, axis, flip):
    size = lax.axis_size(axis)
    return lax.ppermute(value, axis, [(i, i ^ flip) for i in range(size)])


def piece_of(k, width):
    return pl.ds(pl.multiple_of((lax.axis_index("replica") ^ k) * width, width), width)


def tree(parts):
    while len(parts) > 1:
        parts = [parts[i] + parts[i + 1] for i in range(0, len(parts), 2)]
    return parts[0]


def cut_kernel(flips, arrays, *refs):
    grad, sems = refs[0], refs[-1]
    outs = refs[1 + arrays : -1]
    moves = [(grad.at[0, :, piece_of(k, outs[0].shape[1])], out) for k, out in zip(flips, outs)]
    moves += list(zip(refs[1 : 1 + arrays], outs[len(flips) :]))
    copies = [
        pltpu.make_async_copy(source, out, sems.at[i])
        for i, (source, out) in enumerate(moves)
    ]
    for copy in copies:
        copy.start()
    for copy in copies:
        copy.wait()


def cut(grad, width, flips, *arrays):
    piece = jax.ShapeDtypeStruct((grad.shape[1], width), grad.dtype)
    out_shape = [piece] * len(flips) + [jax.ShapeDtypeStruct(x.shape, x.dtype) for x in arrays]
    held = [pltpu.with_memory_space_constraint(x, pltpu.HBM) for x in (grad, *arrays)]
    outs = pl.pallas_call(
        functools.partial(cut_kernel, flips, len(arrays)),
        out_shape=out_shape,
        in_specs=[HBM] * len(held),
        out_specs=[VMEM] * len(out_shape),
        scratch_shapes=[pltpu.SemaphoreType.DMA((len(out_shape),))],
        compiler_params=pltpu.CompilerParams(vmem_limit_bytes=LIMIT),
    )(*held)
    return dict(zip(flips, outs)), outs[len(flips) :]


def average_kernel(groups, *refs):
    pieces, rest = refs[:groups], refs[groups:]
    if len(rest) > 2:
        first, second, average, squares, other_sum = rest
        other_sum[...] = first[...].astype(WIDE) + second[...].astype(WIDE)
    else:
        average, squares = rest
    mean = tree([piece[...].astype(WIDE) for piece in pieces]) / WIDE(groups)
    average[...] = mean
    row = jnp.sum(mean * mean, axis=0, keepdims=True)
    lanes = functools.reduce(
        jnp.add, [row[:, i : i + 128] for i in range(0, row.shape[1], 128)]
    )
    squares[...] = jnp.broadcast_to(lanes[None], squares.shape)


def join_kernel(groups, own, here, first, second, averages):
    there = first[...].astype(WIDE) + second[...].astype(WIDE)
    averages[0] = own[...]
    averages[1] = (here[...] + there) / WIDE(groups)


def factor_kernel(count, squares, factor):
    square_sum = jnp.sum(squares[...], keepdims=True).reshape(1, 1)
    factor[...] = jnp.broadcast_to(0.2 / jnp.sqrt(square_sum / WIDE(count) + 1e-06), factor.shape)


def update_kernel(flips, passed, factor, params, momentum, *refs):
    if len(refs[0].shape) == 3:
        averages, refs = [refs[0][i] for i in range(len(flips))], refs[1 + passed :]
    else:
        averages, refs = [ref[...] for ref in refs[: len(flips)]], refs[len(flips) + passed :]
    new_params, new_momentum, params_out, momentum_out, sems = refs
    width = params_out.shape[2]
    copies = []
    for i, (k, average) in enumerate(zip(flips, averages)):
        cols = piece_of(k, width)
        clipped = factor[:, :1] * average
        fresh = 0.9 * momentum[:, cols] + clipped
        momentum_out[i] = fresh
        params_out[i] = params[:, cols] - 0.7 * (clipped + 0.9 * fresh)
        copies += [
            pltpu.make_async_copy(momentum_out.at[i], new_momentum.at[:, cols], sems.at[0, i]),
            pltpu.make_async_copy(params_out.at[i], new_params.at[:, cols], sems.at[1, i]),
        ]
        copies[-2].start()
        copies[-1].start()
    for copy in copies:
        copy.wait()


def update(flips, averages, factor, params, momentum, earlier=()):
    rows, width = averages[0].shape[-2:]
    out = jax.ShapeDtypeStruct(params.shape, WIDE)
    first = 3 + len(averages)
    return pl.pallas_call(
        functools.partial(update_kernel, flips, len(earlier)),
        out_shape=[out, out],
        in_specs=[VMEM] * first + [HBM] * len(earlier),
        out_specs=[HBM] * 2,
        scratch_shapes=[
            pltpu.VMEM((len(flips), rows, width), WIDE),
            pltpu.VMEM((len(flips), rows, width), WIDE),
            pltpu.SemaphoreType.DMA((2, len(flips))),
        ],
        input_output_aliases={first + i: i for i in range(len(earlier))},
        compiler_params=pltpu.CompilerParams(vmem_limit_bytes=LIMIT),
    )(factor, params, momentum, *averages, *earlier)


def per_device(pseudo_grad, params, momentum):
    groups = lax.axis_size("replica")
    devices = groups * lax.axis_size("fsdp")
    rows, columns = params.shape
    width = columns // groups
    count = rows * lax.axis_size("fsdp") * columns
    limit = pltpu.CompilerParams(vmem_limit_bytes=LIMIT)
    pieces, _ = cut(pseudo_grad, width, range(2, groups))
    pieces, pseudo_grad, params, momentum = lax.optimization_barrier(
        (pieces, pseudo_grad, params, momentum)
    )
    moved = {k: swapped(pieces[k], "replica", k) for k in range(2, groups)}
    near, (params,) = cut(pseudo_grad, width, range(2), params)
    moved.update({0: near[0], 1: swapped(near[1], "replica", 1)})
    again = {}
    if groups == 4:
        near, params, momentum = lax.optimization_barrier((near, params, momentum))
        _, (momentum,) = cut(pseudo_grad, width, (), momentum)
        near, params, momentum = lax.optimization_barrier((near, params, momentum))
        again = {k: swapped(near[k ^ 2], "replica", k) for k in (2, 3)}
        again[1] = swapped(pieces[3], "replica", 1)
    else:
        _, (momentum,) = cut(pseudo_grad, width, (), momentum)
    wide_piece = jax.ShapeDtypeStruct((rows, width), WIDE)
    parts = [moved[k] for k in range(groups)]
    out_shape = [wide_piece, jax.ShapeDtypeStruct((devices, 1, 128), WIDE)]
    if groups == 4:
        parts += [pieces[2], again.pop(1)]
        out_shape += [wide_piece]
    average, squares, *other_sum = pl.pallas_call(
        functools.partial(average_kernel, groups),
        out_shape=out_shape,
        in_specs=[VMEM] * len(parts),
        out_specs=[VMEM] * len(out_shape),
        compiler_params=limit,
    )(*parts)
    averages = {0: average}
    if groups != 4:
        averages.update({k: swapped(average, "replica", k) for k in range(2, groups, 2)})
    squares = lax.all_to_all(
        squares, ("replica", "fsdp"), split_axis=0, concat_axis=0, tiled=True
    )
    factor = pl.pallas_call(
        functools.partial(factor_kernel, count),
        out_shape=jax.ShapeDtypeStruct((1, 128), WIDE),
        in_specs=[VMEM],
        out_specs=VMEM,
        compiler_params=limit,
    )(squares)
    factor, again, averages = lax.optimization_barrier((factor, again, averages))
    if groups == 4:
        joined = pl.pallas_call(
            functools.partial(join_kernel, groups),
            out_shape=jax.ShapeDtypeStruct((2, rows, width), WIDE),
            in_specs=[VMEM] * 4,
            out_specs=VMEM,
            compiler_params=limit,
        )(averages[0], *other_sum, again[2], again[3])
        mates = swapped(joined, "replica", 1)
        outs = update((0, 2), [joined], factor, params, momentum)
        return update((1, 3), [mates], factor, params, momentum, outs)
    for k in range(0, groups, 2):
        averages[k + 1] = swapped(averages[k], "replica", 1)
    here = [k for k in range(groups) if k % 2 == 0]
    late = [k for k in range(groups) if k not in here]
    outs = update(here, [averages[k] for k in here], factor, params, momentum)
    if late:
        outs = update(
            late, [averages[k] for k in late], factor, params, momentum, outs
        )
    return outs


def solution(mesh):
    placed = (P("replica", "fsdp", None), P("fsdp", None), P("fsdp", None))
    return jax.shard_map(
        per_device,
        mesh=mesh,
        in_specs=placed,
        out_specs=(P("fsdp", None), P("fsdp", None)),
        check_vma=False,
    )
```

```python
import functools

import jax
import jax.numpy as jnp
from jax import lax
from jax.experimental import pallas as pl
from jax.experimental.pallas import tpu as pltpu
from jax.sharding import PartitionSpec as P

WIDE = jnp.float32
VMEM = pl.BlockSpec(memory_space=pltpu.VMEM)
HBM = pl.BlockSpec(memory_space=pltpu.HBM)
LIMIT = 16 * 1024 * 1024


def swapped(value, axis, flip):
    size = lax.axis_size(axis)
    return lax.ppermute(value, axis, [(i, i ^ flip) for i in range(size)])


def piece_of(k, width):
    return pl.ds(pl.multiple_of((lax.axis_index("replica") ^ k) * width, width), width)


def tree(parts):
    while len(parts) > 1:
        parts = [parts[i] + parts[i + 1] for i in range(0, len(parts), 2)]
    return parts[0]


def cut_kernel(flips, arrays, *refs):
    grad, sems = refs[0], refs[-1]
    outs = refs[1 + arrays : -1]
    moves = [(grad.at[0, :, piece_of(k, outs[0].shape[1])], out) for k, out in zip(flips, outs)]
    moves += list(zip(refs[1 : 1 + arrays], outs[len(flips) :]))
    copies = [
        pltpu.make_async_copy(source, out, sems.at[i])
        for i, (source, out) in enumerate(moves)
    ]
    for copy in copies:
        copy.start()
    for copy in copies:
        copy.wait()


def cut(grad, width, flips, *arrays):
    piece = jax.ShapeDtypeStruct((grad.shape[1], width), grad.dtype)
    out_shape = [piece] * len(flips) + [jax.ShapeDtypeStruct(x.shape, x.dtype) for x in arrays]
    held = [pltpu.with_memory_space_constraint(x, pltpu.HBM) for x in (grad, *arrays)]
    outs = pl.pallas_call(
        functools.partial(cut_kernel, flips, len(arrays)),
        out_shape=out_shape,
        in_specs=[HBM] * len(held),
        out_specs=[VMEM] * len(out_shape),
        scratch_shapes=[pltpu.SemaphoreType.DMA((len(out_shape),))],
        compiler_params=pltpu.CompilerParams(vmem_limit_bytes=LIMIT),
    )(*held)
    return dict(zip(flips, outs)), outs[len(flips) :]


def average_kernel(groups, *refs):
    pieces, rest = refs[:groups], refs[groups:]
    if len(rest) > 2:
        first, second, average, squares, other_sum = rest
        other_sum[...] = first[...].astype(WIDE) + second[...].astype(WIDE)
    else:
        average, squares = rest
    mean = tree([piece[...].astype(WIDE) for piece in pieces]) / WIDE(groups)
    average[...] = mean
    row = jnp.sum(mean * mean, axis=0, keepdims=True)
    lanes = functools.reduce(
        jnp.add, [row[:, i : i + 128] for i in range(0, row.shape[1], 128)]
    )
    squares[...] = jnp.broadcast_to(lanes[None], squares.shape)


def join_kernel(groups, here, first, second, average):
    there = first[...].astype(WIDE) + second[...].astype(WIDE)
    average[...] = (here[...] + there) / WIDE(groups)


def factor_kernel(count, squares, factor):
    square_sum = jnp.sum(squares[...], keepdims=True).reshape(1, 1)
    factor[...] = jnp.broadcast_to(0.2 / jnp.sqrt(square_sum / WIDE(count) + 1e-06), factor.shape)


def update_kernel(flips, passed, factor, params, momentum, *refs):
    averages, refs = refs[: len(flips)], refs[len(flips) + passed :]
    new_params, new_momentum, params_out, momentum_out, sems = refs
    width = averages[0].shape[1]
    copies = []
    for i, (k, average) in enumerate(zip(flips, averages)):
        cols = piece_of(k, width)
        clipped = factor[:, :1] * average[...]
        fresh = 0.9 * momentum[:, cols] + clipped
        momentum_out[i] = fresh
        params_out[i] = params[:, cols] - 0.7 * (clipped + 0.9 * fresh)
        copies += [
            pltpu.make_async_copy(momentum_out.at[i], new_momentum.at[:, cols], sems.at[0, i]),
            pltpu.make_async_copy(params_out.at[i], new_params.at[:, cols], sems.at[1, i]),
        ]
        copies[-2].start()
        copies[-1].start()
    for copy in copies:
        copy.wait()


def update(flips, averages, factor, params, momentum, earlier=()):
    rows, width = averages[0].shape
    out = jax.ShapeDtypeStruct(params.shape, WIDE)
    first = 3 + len(flips)
    return pl.pallas_call(
        functools.partial(update_kernel, flips, len(earlier)),
        out_shape=[out, out],
        in_specs=[VMEM] * first + [HBM] * len(earlier),
        out_specs=[HBM] * 2,
        scratch_shapes=[
            pltpu.VMEM((len(flips), rows, width), WIDE),
            pltpu.VMEM((len(flips), rows, width), WIDE),
            pltpu.SemaphoreType.DMA((2, len(flips))),
        ],
        input_output_aliases={first + i: i for i in range(len(earlier))},
        compiler_params=pltpu.CompilerParams(vmem_limit_bytes=LIMIT),
    )(factor, params, momentum, *averages, *earlier)


def per_device(pseudo_grad, params, momentum):
    groups = lax.axis_size("replica")
    devices = groups * lax.axis_size("fsdp")
    rows, columns = params.shape
    width = columns // groups
    count = rows * lax.axis_size("fsdp") * columns
    limit = pltpu.CompilerParams(vmem_limit_bytes=LIMIT)
    pieces, _ = cut(pseudo_grad, width, range(2, groups))
    pieces, pseudo_grad, params, momentum = lax.optimization_barrier(
        (pieces, pseudo_grad, params, momentum)
    )
    moved = {k: swapped(pieces[k], "replica", k) for k in range(2, groups)}
    near, (params, momentum) = cut(pseudo_grad, width, range(2), params, momentum)
    moved.update({0: near[0], 1: swapped(near[1], "replica", 1)})
    again = {}
    if groups == 4:
        again = {k: swapped(near[k ^ 2], "replica", k) for k in (2, 3)}
        again[1] = swapped(pieces[3], "replica", 1)
    wide_piece = jax.ShapeDtypeStruct((rows, width), WIDE)
    parts = [moved[k] for k in range(groups)]
    out_shape = [wide_piece, jax.ShapeDtypeStruct((devices, 1, 128), WIDE)]
    if groups == 4:
        parts += [pieces[2], again.pop(1)]
        out_shape += [wide_piece]
    average, squares, *other_sum = pl.pallas_call(
        functools.partial(average_kernel, groups),
        out_shape=out_shape,
        in_specs=[VMEM] * len(parts),
        out_specs=[VMEM] * len(out_shape),
        compiler_params=limit,
    )(*parts)
    averages = {0: average}
    if groups != 4:
        averages.update({k: swapped(average, "replica", k) for k in range(2, groups, 2)})
    squares = lax.all_to_all(
        squares, ("replica", "fsdp"), split_axis=0, concat_axis=0, tiled=True
    )
    factor = pl.pallas_call(
        functools.partial(factor_kernel, count),
        out_shape=jax.ShapeDtypeStruct((1, 128), WIDE),
        in_specs=[VMEM],
        out_specs=VMEM,
        compiler_params=limit,
    )(squares)
    factor, again = lax.optimization_barrier((factor, again))
    if groups == 4:
        averages[2] = pl.pallas_call(
            functools.partial(join_kernel, groups),
            out_shape=wide_piece,
            in_specs=[VMEM] * 3,
            out_specs=VMEM,
            compiler_params=limit,
        )(*other_sum, again[2], again[3])
    factor, averages = lax.optimization_barrier((factor, averages))
    for k in range(0, groups, 2):
        averages[k + 1] = swapped(averages[k], "replica", 1)
    here = [k for k in range(groups) if k % 2 == 0]
    late = [k for k in range(groups) if k not in here]
    outs = update(here, [averages[k] for k in here], factor, params, momentum)
    if late:
        outs = update(
            late, [averages[k] for k in late], factor, params, momentum, outs
        )
    return outs


def solution(mesh):
    placed = (P("replica", "fsdp", None), P("fsdp", None), P("fsdp", None))
    return jax.shard_map(
        per_device,
        mesh=mesh,
        in_specs=placed,
        out_specs=(P("fsdp", None), P("fsdp", None)),
        check_vma=False,
    )
```

```python
import functools

import jax
import jax.numpy as jnp
from jax import lax
from jax.experimental import pallas as pl
from jax.experimental.pallas import tpu as pltpu
from jax.sharding import PartitionSpec as P

WIDE = jnp.float32
VMEM = pl.BlockSpec(memory_space=pltpu.VMEM)
HBM = pl.BlockSpec(memory_space=pltpu.HBM)
LIMIT = 16 * 1024 * 1024


def swapped(value, axis, flip):
    size = lax.axis_size(axis)
    return lax.ppermute(value, axis, [(i, i ^ flip) for i in range(size)])


def piece_of(k, width):
    return pl.ds(pl.multiple_of((lax.axis_index("replica") ^ k) * width, width), width)


def tree(parts):
    while len(parts) > 1:
        parts = [parts[i] + parts[i + 1] for i in range(0, len(parts), 2)]
    return parts[0]


def cut_kernel(flips, arrays, *refs):
    grad, sems = refs[0], refs[-1]
    outs = refs[1 + arrays : -1]
    moves = [(grad.at[0, :, piece_of(k, outs[0].shape[1])], out) for k, out in zip(flips, outs)]
    moves += list(zip(refs[1 : 1 + arrays], outs[len(flips) :]))
    copies = [
        pltpu.make_async_copy(source, out, sems.at[i])
        for i, (source, out) in enumerate(moves)
    ]
    for copy in copies:
        copy.start()
    for copy in copies:
        copy.wait()


def cut(grad, width, flips, *arrays):
    piece = jax.ShapeDtypeStruct((grad.shape[1], width), grad.dtype)
    out_shape = [piece] * len(flips) + [jax.ShapeDtypeStruct(x.shape, x.dtype) for x in arrays]
    held = [pltpu.with_memory_space_constraint(x, pltpu.HBM) for x in (grad, *arrays)]
    outs = pl.pallas_call(
        functools.partial(cut_kernel, flips, len(arrays)),
        out_shape=out_shape,
        in_specs=[HBM] * len(held),
        out_specs=[VMEM] * len(out_shape),
        scratch_shapes=[pltpu.SemaphoreType.DMA((len(out_shape),))],
        compiler_params=pltpu.CompilerParams(vmem_limit_bytes=LIMIT),
    )(*held)
    return dict(zip(flips, outs)), outs[len(flips) :]


def average_kernel(groups, *refs):
    pieces, rest = refs[:groups], refs[groups:]
    if len(rest) > 2:
        first, second, average, squares, other_sum = rest
        other_sum[...] = first[...].astype(WIDE) + second[...].astype(WIDE)
    else:
        average, squares = rest
    mean = tree([piece[...].astype(WIDE) for piece in pieces]) / WIDE(groups)
    average[...] = mean
    row = jnp.sum(mean * mean, axis=0, keepdims=True)
    lanes = functools.reduce(
        jnp.add, [row[:, i : i + 128] for i in range(0, row.shape[1], 128)]
    )
    squares[...] = jnp.broadcast_to(lanes[None], squares.shape)


def join_kernel(groups, here, first, second, average):
    there = first[...].astype(WIDE) + second[...].astype(WIDE)
    average[...] = (here[...] + there) / WIDE(groups)


def factor_kernel(count, squares, factor):
    square_sum = jnp.sum(squares[...], keepdims=True).reshape(1, 1)
    factor[...] = jnp.broadcast_to(0.2 / jnp.sqrt(square_sum / WIDE(count) + 1e-06), factor.shape)


def update_kernel(flips, passed, factor, params, momentum, *refs):
    averages, refs = refs[: len(flips)], refs[len(flips) + passed :]
    new_params, new_momentum, params_out, momentum_out, sems = refs
    width = averages[0].shape[1]
    copies = []
    for i, (k, average) in enumerate(zip(flips, averages)):
        cols = piece_of(k, width)
        clipped = factor[:, :1] * average[...]
        fresh = 0.9 * momentum[:, cols] + clipped
        momentum_out[i] = fresh
        params_out[i] = params[:, cols] - 0.7 * (clipped + 0.9 * fresh)
        copies += [
            pltpu.make_async_copy(momentum_out.at[i], new_momentum.at[:, cols], sems.at[0, i]),
            pltpu.make_async_copy(params_out.at[i], new_params.at[:, cols], sems.at[1, i]),
        ]
        copies[-2].start()
        copies[-1].start()
    for copy in copies:
        copy.wait()


def update(flips, averages, factor, params, momentum, earlier=()):
    rows, width = averages[0].shape
    out = jax.ShapeDtypeStruct(params.shape, WIDE)
    first = 3 + len(flips)
    return pl.pallas_call(
        functools.partial(update_kernel, flips, len(earlier)),
        out_shape=[out, out],
        in_specs=[VMEM] * first + [HBM] * len(earlier),
        out_specs=[HBM] * 2,
        scratch_shapes=[
            pltpu.VMEM((len(flips), rows, width), WIDE),
            pltpu.VMEM((len(flips), rows, width), WIDE),
            pltpu.SemaphoreType.DMA((2, len(flips))),
        ],
        input_output_aliases={first + i: i for i in range(len(earlier))},
        compiler_params=pltpu.CompilerParams(vmem_limit_bytes=LIMIT),
    )(factor, params, momentum, *averages, *earlier)


def per_device(pseudo_grad, params, momentum):
    groups = lax.axis_size("replica")
    devices = groups * lax.axis_size("fsdp")
    rows, columns = params.shape
    width = columns // groups
    count = rows * lax.axis_size("fsdp") * columns
    limit = pltpu.CompilerParams(vmem_limit_bytes=LIMIT)
    pieces, _ = cut(pseudo_grad, width, range(2, groups))
    pieces, pseudo_grad, params, momentum = lax.optimization_barrier(
        (pieces, pseudo_grad, params, momentum)
    )
    moved = {k: swapped(pieces[k], "replica", k) for k in range(2, groups)}
    near, (params,) = cut(pseudo_grad, width, range(2), params)
    moved.update({0: near[0], 1: swapped(near[1], "replica", 1)})
    again = {}
    if groups == 4:
        near, params, momentum = lax.optimization_barrier((near, params, momentum))
        _, (momentum,) = cut(pseudo_grad, width, (), momentum)
        near, params, momentum = lax.optimization_barrier((near, params, momentum))
        again = {k: swapped(near[k ^ 2], "replica", k) for k in (2, 3)}
        again[1] = swapped(pieces[3], "replica", 1)
    else:
        _, (momentum,) = cut(pseudo_grad, width, (), momentum)
    wide_piece = jax.ShapeDtypeStruct((rows, width), WIDE)
    parts = [moved[k] for k in range(groups)]
    out_shape = [wide_piece, jax.ShapeDtypeStruct((devices, 1, 128), WIDE)]
    if groups == 4:
        parts += [pieces[2], again.pop(1)]
        out_shape += [wide_piece]
    average, squares, *other_sum = pl.pallas_call(
        functools.partial(average_kernel, groups),
        out_shape=out_shape,
        in_specs=[VMEM] * len(parts),
        out_specs=[VMEM] * len(out_shape),
        compiler_params=limit,
    )(*parts)
    averages = {0: average}
    if groups != 4:
        averages.update({k: swapped(average, "replica", k) for k in range(2, groups, 2)})
    squares = lax.all_to_all(
        squares, ("replica", "fsdp"), split_axis=0, concat_axis=0, tiled=True
    )
    squares, averages = lax.optimization_barrier((squares, averages))
    own_forward = swapped(averages[0], "replica", 1)
    factor = pl.pallas_call(
        functools.partial(factor_kernel, count),
        out_shape=jax.ShapeDtypeStruct((1, 128), WIDE),
        in_specs=[VMEM],
        out_specs=VMEM,
        compiler_params=limit,
    )(squares)
    factor, again = lax.optimization_barrier((factor, again))
    if groups == 4:
        averages[2] = pl.pallas_call(
            functools.partial(join_kernel, groups),
            out_shape=wide_piece,
            in_specs=[VMEM] * 3,
            out_specs=VMEM,
            compiler_params=limit,
        )(*other_sum, again[2], again[3])
    factor, averages = lax.optimization_barrier((factor, averages))
    averages[1] = own_forward
    for k in range(2, groups, 2):
        averages[k + 1] = swapped(averages[k], "replica", 1)
    here = [k for k in range(groups) if k % 2 == 0]
    late = [k for k in range(groups) if k not in here]
    outs = update(here, [averages[k] for k in here], factor, params, momentum)
    if late:
        outs = update(
            late, [averages[k] for k in late], factor, params, momentum, outs
        )
    return outs


def solution(mesh):
    placed = (P("replica", "fsdp", None), P("fsdp", None), P("fsdp", None))
    return jax.shard_map(
        per_device,
        mesh=mesh,
        in_specs=placed,
        out_specs=(P("fsdp", None), P("fsdp", None)),
        check_vma=False,
    )
```
